128 devices in a mesh: rep: 8 (over z, core), fsdp: 16 (over y, x).
Axes of the slice: x: 4, y: 4, z: 4, core: 2. Of those that a mesh axis runs over, the one named last changes fastest.
Arguments:
- partials: bfloat16 [8, 16, 64, 131072], P('rep', 'fsdp'), may hold values from -5 to 5
- momentum: float32 [8, 64, 131072], P('rep', None, 'fsdp'), may hold values from -6 to 6
- positions: int32 [8, 8, 131072], P('rep', None, 'fsdp'), may hold values from 0 to 63, as said below
Outputs:
- update: float32 [64, 131072], P(None, 'fsdp')
- new_momentum: float32 [8, 64, 131072], P('rep', None, 'fsdp')
The draws below stay inside these ranges and needn't reach their ends.
Inputs may be any that keep to these rules, and one draw needn't show every extreme that they name: For each replica and span the 8 positions are different numbers.
All inputs are finite; a program needn't handle non-finite values.
Results may differ from the reference program's by a relative error of at most 0.0003.
Values sent between devices are 32-bit elements; how exact they have to be, the bound alone decides.
No kernel may reach another device: no remote copies, remote signals or barrier semaphores. Data moves between devices by JAX's collectives and lax.ppermute only.
A program may use at most 128 MiB of HBM per device.

```python
import jax
import jax.numpy as jnp
from jax import lax

BLOCK = 64
KEEP = 8
SPANS = 131072
N_REP = 8
N_FSDP = 16


def draw_positions(key, part):
    key = jax.random.fold_in(key, 7)
    scores = jax.random.randint(key, (N_REP, SPANS, BLOCK), 0, 1 << 20) * BLOCK
    scores = scores + jnp.arange(BLOCK, dtype=jnp.int32)[None, None, :]
    picked = lax.top_k(scores, KEEP)[1].astype(jnp.int32)
    return jnp.transpose(picked, (0, 2, 1))


def spiked(drawn, own_key, source, target, parts, factor):
    owner, partner = [(jnp.arange(drawn.shape[dim]) // (drawn.shape[dim] // parts)).reshape([-1 if axis == dim else 1 for axis in range(drawn.ndim)]) for dim in (source, target)]
    chosen = jax.random.permutation(own_key, parts)[partner]
    strong = (owner == chosen) | (owner == (partner + parts // 2) % parts)
    return jnp.where(strong, factor * drawn, drawn)


def block_scale(own_key, extent, split, least, largest):
    level, own = 1.0, jax.random.fold_in(own_key, 6)
    for position, parts in split:
        heights = jnp.exp(jax.random.uniform(jax.random.fold_in(own, position), (parts,), jnp.float32, least / len(split), largest / len(split)))
        level = level * jnp.repeat(heights, extent[position] // parts).reshape([-1 if axis == position else 1 for axis in range(len(extent))])
    return level


def normal_values(rng, shape, deviation, bound, cuts=(), kind=jnp.bfloat16):
    level = block_scale(rng, shape, cuts, -0.22, 0.18) if cuts else 1.0
    values = jax.random.normal(rng, shape, jnp.float32) * deviation * level
    return jnp.minimum(jnp.maximum(values, -bound), bound).astype(kind)


def gaussian_with(own_key, extent, spread, limit, split, heavy, kind=jnp.bfloat16):
    values = spread * jax.random.normal(own_key, extent, jnp.float32)
    if split:
        values = values * block_scale(own_key, extent, split, -0.22, 0.18)
    return jnp.clip(spiked(values, jax.random.fold_in(own_key, 3), *heavy), -limit, limit).astype(kind)


def setup_inputs(seed: int = 0) -> dict:
    streams_of = jax.random.split(jax.random.key(seed), 4)
    partials = gaussian_with(streams_of[0], (N_REP, N_FSDP, BLOCK, SPANS), 0.25, 5.0, ((0, 8), (1, 16)), (1, 3, 16, 2.0))
    momentum = normal_values(streams_of[1], (N_REP, BLOCK, SPANS), 1.0, 6.0, ((0, 8), (2, 16)), jnp.float32)
    positions = draw_positions(jax.random.fold_in(streams_of[3], 71), 0)
    return {"partials": partials, "momentum": momentum, "positions": positions}


def dct_matrix():
    freq = jnp.arange(BLOCK).astype(jnp.float32)[:, None]
    place = jnp.arange(BLOCK).astype(jnp.float32)[None, :]
    basis = jnp.cos(jnp.pi * (2.0 * place + 1.0) * freq / (2.0 * BLOCK))
    scale = jnp.where(freq == 0.0, jnp.sqrt(1.0 / BLOCK), jnp.sqrt(2.0 / BLOCK))
    return (scale * basis).astype(jnp.float32)

def one_replica(args):
    part, moment_old, chosen = args
    dct = dct_matrix()
    grad = lax.optimization_barrier(jnp.sum(part.astype(jnp.float32), axis=0))
    moment = 0.9 * moment_old + grad
    coeff = jnp.dot(dct, moment, precision=lax.Precision.HIGHEST, preferred_element_type=jnp.float32)
    freq = jnp.arange(BLOCK).astype(jnp.int32)
    keep = jnp.any(chosen[:, None, :] == freq[None, :, None], axis=0)
    own = jnp.where(keep, coeff, 0.0)
    fresh = moment - jnp.dot(dct.T, own, precision=lax.Precision.HIGHEST, preferred_element_type=jnp.float32)
    return (own, fresh)

def reference(partials, momentum, positions):
    own, new_momentum = lax.map(one_replica, (partials, momentum, positions))
    total = lax.optimization_barrier(jnp.sum(own, axis=0))
    update = jnp.dot(dct_matrix().T, total, precision=lax.Precision.HIGHEST, preferred_element_type=jnp.float32)
    return (update, new_momentum)
```

```python
import functools

import jax
import jax.numpy as jnp
import ml_dtypes
import numpy as np
from jax import lax
from jax.experimental import pallas as pl
from jax.experimental.pallas import tpu as pltpu
from jax.sharding import PartitionSpec as P

BLOCK = 64
HALF = BLOCK // 2
KEEP = 8
SIDE = 4
WIDTHS = (2048, 1024, 1024)
VMEM_LIMIT = 48 * 1024 * 1024
F32 = jnp.float32
BF16 = jnp.bfloat16


def dct_parts():
    k = np.arange(BLOCK, dtype=np.float64)[:, None]
    n = np.arange(BLOCK, dtype=np.float64)[None, :]
    scale = np.where(k == 0, np.sqrt(1.0 / BLOCK), np.sqrt(2.0 / BLOCK))
    dct = scale * np.cos(np.pi * (2.0 * n + 1.0) * k / (2.0 * BLOCK))

    def wide(mat):
        high = mat.astype(ml_dtypes.bfloat16)
        low = (mat - high.astype(np.float64)).astype(ml_dtypes.bfloat16)
        return np.concatenate([high, high, low, low], axis=1)

    return wide(dct), wide(dct.T.copy())


def params():
    return pltpu.CompilerParams(vmem_limit_bytes=VMEM_LIMIT)


def cost(flops, nbytes):
    return pl.CostEstimate(flops=flops, bytes_accessed=nbytes, transcendentals=0)


def fold(coord, step):
    return lax.rem(coord + (step + SIDE), SIDE)


class Half:
    def __init__(self, x_first, offset, width, spans):
        self.x_first = x_first
        self.width = width
        self.first = offset // width
        self.per_target = spans // width

    def column(self, here, step, other):
        y, x = here[0], here[1]
        if self.x_first:
            target = other * SIDE + fold(x, step)
        else:
            target = fold(y, step) * SIDE + other
        return target * self.per_target + self.first

    def second(self, here, step):
        return fold(here[0] if self.x_first else here[1], step)

    def grid_block(self, step):
        return pl.BlockSpec((BLOCK, self.width), lambda i, here: (0, self.column(here, step, i)))

    def one_block(self, step):
        return pl.BlockSpec(
            (BLOCK, self.width), lambda i, here: (0, self.column(here, 0, self.second(here, step)))
        )

    def message_block(self, step):
        return pl.BlockSpec((1, BLOCK, self.width), lambda i, here: (self.second(here, step), 0, 0))


def whole(*shape):
    return pl.BlockSpec(shape, lambda i, here: (0,) * len(shape))


def call(body, grid, here, ins, in_specs, out_shape, out_specs, nbytes, flops=0, aliases=None, scratch=()):
    return pl.pallas_call(
        body,
        grid_spec=pltpu.PrefetchScalarGridSpec(
            num_scalar_prefetch=1,
            grid=(grid,),
            in_specs=in_specs,
            out_specs=out_specs,
            scratch_shapes=scratch,
        ),
        out_shape=out_shape,
        input_output_aliases=aliases or {},
        compiler_params=params(),
        cost_estimate=cost(flops, nbytes),
    )(here, *ins)


def far_body(here, part, up, down):
    up[0] = part[:HALF].astype(F32)
    down[0] = part[HALF:].astype(F32)


def send_far(half, here, partials):
    w = half.width
    shape = jax.ShapeDtypeStruct((SIDE, HALF, w), F32)
    spec = pl.BlockSpec((1, HALF, w), lambda i, here: (i, 0, 0))
    return call(
        far_body, SIDE, here, (partials,), [half.grid_block(2)], (shape, shape), (spec, spec),
        SIDE * BLOCK * w * 6,
    )


def near_body(here, part_up, part_down, got_up, got_down, up, down):
    up[0, :HALF] = part_up[:HALF].astype(F32) + got_up[0]
    up[0, HALF:] = part_up[HALF:].astype(F32)
    down[0, :HALF] = part_down[:HALF].astype(F32)
    down[0, HALF:] = part_down[HALF:].astype(F32) + got_down[0]


def send_near(half, here, partials, got_up, got_down):
    w = half.width
    shape = jax.ShapeDtypeStruct((SIDE, BLOCK, w), F32)
    got = pl.BlockSpec((1, HALF, w), lambda i, here: (i, 0, 0))
    spec = pl.BlockSpec((1, BLOCK, w), lambda i, here: (i, 0, 0))
    return call(
        near_body, SIDE, here, (partials, partials, got_up, got_down),
        [half.grid_block(1), half.grid_block(-1), got, got], (shape, shape), (spec, spec),
        SIDE * BLOCK * w * 16,
    )


def far2_body(here, part, left, right, up, down):
    up[...] = part[:HALF].astype(F32) + left[0, :HALF] + right[0, :HALF]
    down[...] = part[HALF:].astype(F32) + left[0, HALF:] + right[0, HALF:]


def send_far2(half, here, partials, left, right):
    w = half.width
    shape = jax.ShapeDtypeStruct((HALF, w), F32)
    return call(
        far2_body, 1, here, (partials, left, right),
        [half.one_block(2), half.message_block(2), half.message_block(2)],
        (shape, shape), (whole(HALF, w), whole(HALF, w)), BLOCK * w * 14,
    )


def near2_body(here, part_u, left_u, right_u, part_d, left_d, right_d, got_up, got_down, up, down):
    up[:HALF] = part_u[:HALF].astype(F32) + left_u[0, :HALF] + right_u[0, :HALF] + got_up[...]
    up[HALF:] = part_u[HALF:].astype(F32) + left_u[0, HALF:] + right_u[0, HALF:]
    down[:HALF] = part_d[:HALF].astype(F32) + left_d[0, :HALF] + right_d[0, :HALF]
    down[HALF:] = part_d[HALF:].astype(F32) + left_d[0, HALF:] + right_d[0, HALF:] + got_down[...]


def send_near2(half, here, partials, left, right, got_up, got_down):
    w = half.width
    shape = jax.ShapeDtypeStruct((BLOCK, w), F32)
    return call(
        near2_body, 1, here, (partials, left, right, partials, left, right, got_up, got_down),
        [half.one_block(1), half.message_block(1), half.message_block(1),
         half.one_block(-1), half.message_block(-1), half.message_block(-1),
         whole(HALF, w), whole(HALF, w)],
        (shape, shape), (whole(BLOCK, w), whole(BLOCK, w)), BLOCK * w * 32,
    )


def product(parts, value):
    high = value.astype(BF16)
    low = (value - high.astype(F32)).astype(BF16)
    return jnp.dot(
        parts, jnp.concatenate([high, low, high, low], axis=0), preferred_element_type=F32
    )


def finish_body(step, here, *refs):
    halves, (momentum, positions, forward, backward) = (refs[0:5], refs[5:10]), refs[10:14]
    fresh, values = refs[-2:]
    w = halves[0][0].shape[1]
    freq = lax.broadcasted_iota(jnp.int32, (BLOCK, step), 0)
    for number, (part, left, right, left2, right2) in enumerate(halves):

        @pl.loop(0, w // step)
        def _(tile):
            col = pl.ds(pl.multiple_of(tile * step, step), step)
            out = pl.ds(pl.multiple_of(number * w + tile * step, step), step)
            grad = part[:, col].astype(F32) + left[0, :, col] + right[0, :, col]
            grad = grad + left2[:, col] + right2[:, col]
            moment = 0.9 * momentum[0, :, out] + grad
            coeff = product(forward[...], moment)
            chosen = positions[0, :, out]
            own = jnp.zeros_like(coeff)
            rows = []
            for place in range(KEEP):
                hit = jnp.where(chosen[place : place + 1] == freq, coeff, 0.0)
                rows.append(jnp.sum(hit, axis=0, keepdims=True))
                own = own + hit
            values[:, out] = jnp.concatenate(rows, axis=0)
            fresh[0, :, out] = moment - product(backward[...], own)


def finish(pair, piece, here, partials, momentum, positions, got, tables, fresh_so_far):
    w = pair[0].width
    ins, specs = [], []
    for half, (left, right, left2, right2) in zip(pair, got):
        ins += [partials, left, right, left2, right2]
        specs += [half.one_block(0), half.message_block(0), half.message_block(0),
                  whole(BLOCK, w), whole(BLOCK, w)]
    ins += [momentum, positions, *tables]
    specs += [
        pl.BlockSpec((1, BLOCK, 2 * w), lambda i, here: (0, 0, piece)),
        pl.BlockSpec((1, KEEP, 2 * w), lambda i, here: (0, 0, piece)),
        whole(BLOCK, 4 * BLOCK),
        whole(BLOCK, 4 * BLOCK),
    ]
    aliases = {}
    if fresh_so_far is not None:
        ins.append(fresh_so_far)
        specs.append(pl.BlockSpec(memory_space=pl.ANY))
        aliases = {len(ins): 0}
    return call(
        functools.partial(finish_body, min(w, 512)), 1, here, ins, specs,
        (jax.ShapeDtypeStruct(momentum.shape, F32), jax.ShapeDtypeStruct((KEEP, 2 * w), F32)),
        (pl.BlockSpec((1, BLOCK, 2 * w), lambda i, here: (0, 0, piece)), whole(KEEP, 2 * w)),
        BLOCK * w * 2 * 26, flops=2 * 2 * BLOCK * 4 * BLOCK * w * 2, aliases=aliases,
    )


def spread_body(step, here, v0, v1, v2, v3, p0, p1, p2, p3, backward, out):
    freq = lax.broadcasted_iota(jnp.int32, (BLOCK, step), 0)

    @pl.loop(0, out.shape[1] // step)
    def _(tile):
        col = pl.ds(pl.multiple_of(tile * step, step), step)
        dense = []
        for vals, pos in ((v0, p0), (v1, p1), (v2, p2), (v3, p3)):
            row, chosen = vals[:, col], pos[0, :, col]
            acc = jnp.zeros((BLOCK, step), F32)
            for place in range(KEEP):
                acc = jnp.where(chosen[place : place + 1] == freq, row[place : place + 1], acc)
            dense.append(acc)
        total = (dense[0] + dense[1]) + (dense[2] + dense[3])
        out[:, col] = product(backward[...], total)


def spread(width, piece, here, vals, pos, table):
    spec = pl.BlockSpec((1, KEEP, width), lambda i, here: (0, 0, piece))
    return call(
        functools.partial(spread_body, min(width, 512)), 1, here, (*vals, *pos, table),
        [whole(KEEP, width)] * 4 + [spec] * 4 + [whole(BLOCK, 4 * BLOCK)],
        jax.ShapeDtypeStruct((BLOCK, width), F32), whole(BLOCK, width),
        width * 4 * (BLOCK + 64), flops=2 * BLOCK * 4 * BLOCK * width,
    )


def join_body(here, mine, other, *refs):
    refs[-1][...] = mine[...] + other[...]


def join(width, piece, here, mine, other, spans, so_far):
    ins, specs, aliases = [mine, other], [whole(BLOCK, width)] * 2, {}
    if so_far is not None:
        ins.append(so_far)
        specs.append(pl.BlockSpec(memory_space=pl.ANY))
        aliases = {3: 0}
    return call(
        join_body, 1, here, ins, specs, jax.ShapeDtypeStruct((BLOCK, spans), F32),
        pl.BlockSpec((BLOCK, width), lambda i, here: (0, piece)), BLOCK * width * 12, aliases=aliases,
    )


def shift(dy, dx):
    return [
        (y * SIDE + x, (y + dy) % SIDE * SIDE + (x + dx) % SIDE)
        for y in range(SIDE)
        for x in range(SIDE)
    ]


def along(x_first, value, step):
    return lax.ppermute(value, "fsdp", shift(0, step) if x_first else shift(step, 0))


def along_z(value, step):
    return lax.ppermute(
        value, "rep", [(z * 2 + c, (z + step) % SIDE * 2 + c) for z in range(SIDE) for c in range(2)]
    )


def other_core(value):
    return lax.ppermute(value, "rep", [(r, r ^ 1) for r in range(2 * SIDE)])


def both(x_first, up, down):
    return along(x_first, up, 1), along(x_first, down, -1)


def on_device(partials, momentum, positions):
    spans = momentum.shape[2]
    flat = partials.reshape(partials.shape[2:])
    me = lax.axis_index("fsdp")
    here = jnp.stack([me // SIDE, lax.rem(me, SIDE)]).astype(jnp.int32)
    forward, backward = (jnp.asarray(part) for part in dct_parts())

    pairs, pieces, start = [], [], 0
    for width in WIDTHS:
        pairs.append((Half(True, start, width, spans), Half(False, start + width, width, spans)))
        pieces.append(start // (2 * width))
        start += 2 * width

    count = len(pairs)
    far, near, far2, near2 = ([[None, None] for _ in pairs] for _ in range(4))
    pos = [positions] + [along_z(positions, step) for step in (2, 1, -1)]
    fresh = update = None
    for stage in range(count + 4):
        for p in range(count):
            phase = stage - p
            for h, half in enumerate(pairs[p]):
                xf = half.x_first
                if phase == 0:
                    far[p][h] = both(xf, *send_far(half, here, flat))
                elif phase == 1:
                    near[p][h] = both(xf, *send_near(half, here, flat, *far[p][h]))
                elif phase == 2:
                    far2[p][h] = both(not xf, *send_far2(half, here, flat, *near[p][h]))
                elif phase == 3:
                    near2[p][h] = both(
                        not xf, *send_near2(half, here, flat, *near[p][h], *far2[p][h])
                    )
            if phase == 4:
                got = [near[p][h] + near2[p][h] for h in range(2)]
                fresh, vals = finish(
                    pairs[p], pieces[p], here, flat, momentum, positions, got, (forward, backward), fresh
                )
                gathered = [vals] + [along_z(vals, step) for step in (2, 1, -1)]
                mine = spread(2 * WIDTHS[p], pieces[p], here, gathered, pos, backward)
                update = join(2 * WIDTHS[p], pieces[p], here, mine, other_core(mine), spans, update)
    return update, fresh


def solution(mesh):
    placed = (P("rep", "fsdp", None, None), P("rep", None, "fsdp"), P("rep", None, "fsdp"))
    return jax.shard_map(
        on_device,
        mesh=mesh,
        in_specs=placed,
        out_specs=(P(None, "fsdp"), P("rep", None, "fsdp")),
        check_vma=False,
    )
```

```python
import jax
import jax.numpy as jnp
import ml_dtypes
import numpy as np
from jax import lax
from jax.experimental import pallas as pl
from jax.experimental.pallas import tpu as pltpu
from jax.sharding import PartitionSpec as P

BLOCK = 64
HALF = BLOCK // 2
KEEP = 8
SIDE = 4
TILE = 512
PIECES = {"a": (0, 2560), "b": (5120, 1536)}
ORDER = "a1 a2 a3 b1 b2a b3 a5 b4 a6 b5 a7 b6 a8 b7 b8"
PLACES_WITH = ("a2", "a3", "b1")
VMEM_LIMIT = 48 * 1024 * 1024
F32 = jnp.float32
BF16 = jnp.bfloat16


def dct_parts():
    k = np.arange(BLOCK, dtype=np.float64)[:, None]
    n = np.arange(BLOCK, dtype=np.float64)[None, :]
    scale = np.where(k == 0, np.sqrt(1.0 / BLOCK), np.sqrt(2.0 / BLOCK))
    dct = scale * np.cos(np.pi * (2.0 * n + 1.0) * k / (2.0 * BLOCK))

    def wide(mat):
        high = mat.astype(ml_dtypes.bfloat16)
        low = (mat - high.astype(np.float64)).astype(ml_dtypes.bfloat16)
        return np.concatenate([high, high, low, low], axis=1)

    return wide(dct), wide(dct.T.copy())


def fold(coord, step):
    return lax.rem(coord + (step + SIDE), SIDE)


class Half:
    def __init__(self, x_first, start, width, spans):
        self.x_first = x_first
        self.width = width
        self.count = width // TILE
        self.first = start // TILE
        self.per_target = spans // TILE

    def column(self, here, step, other):
        y, x = here[0], here[1]
        if self.x_first:
            target = other * SIDE + fold(x, step)
        else:
            target = fold(y, step) * SIDE + other
        return target * self.per_target + self.first

    def second(self, here, step):
        return fold(here[0] if self.x_first else here[1], step)

    def grid_blocks(self, step, rows):
        def spec(tile):
            return pl.BlockSpec(
                (HALF, TILE), lambda i, here: (rows, self.column(here, step, i) + tile)
            )

        return [spec(tile) for tile in range(self.count)]

    def one_blocks(self, step):
        def spec(tile):
            return pl.BlockSpec(
                (BLOCK, TILE),
                lambda i, here: (0, self.column(here, 0, self.second(here, step)) + tile),
            )

        return [spec(tile) for tile in range(self.count)]

    def message_blocks(self, step):
        def spec(tile):
            return pl.BlockSpec(
                (HALF, TILE), lambda i, here: (0, self.second(here, step) * self.count + tile)
            )

        return [spec(tile) for tile in range(self.count)]


def whole(*shape):
    return pl.BlockSpec(shape, lambda i, here: (0,) * len(shape))


class Line:
    def __init__(self, here):
        self.here = here
        self.token = None
        self.arrived = []

    def call(self, body, grid, ins, in_specs, out_shape, out_specs, aliases=None):
        ins, in_specs = list(ins), list(in_specs)
        count = len(ins)
        order = ([] if self.token is None else [self.token]) + self.arrived
        taken = len(order)
        ins += order
        in_specs += [whole(*(1,) * (array.ndim - 2), 8, 128) for array in order]

        def run(here, *refs):
            refs[-1][...] = jnp.zeros((8, 128), F32)
            body(here, *refs[:count], *refs[count + taken : -1])

        *outs, self.token = pl.pallas_call(
            run,
            grid_spec=pltpu.PrefetchScalarGridSpec(
                num_scalar_prefetch=1,
                grid=(grid,),
                in_specs=in_specs,
                out_specs=(*out_specs, whole(8, 128)),
            ),
            out_shape=(*out_shape, jax.ShapeDtypeStruct((8, 128), F32)),
            input_output_aliases=aliases or {},
            compiler_params=pltpu.CompilerParams(vmem_limit_bytes=VMEM_LIMIT),
            cost_estimate=pl.CostEstimate(flops=0, bytes_accessed=0, transcendentals=0),
        )(self.here, *ins)
        return outs


def tiles(n, *groups):
    for tile in range(n):
        yield slice(tile * TILE, (tile + 1) * TILE), [group[tile] for group in groups]


def groups(refs, n):
    return [refs[k : k + n] for k in range(0, len(refs), n)]


def send_part(line, half, partials, up_from, down_from, extra):
    w, n = half.width, half.count

    def body(here, *refs):
        up, down = refs[2 * n :]
        for col, (part_up, part_down) in tiles(n, *groups(refs[: 2 * n], n)):
            up[:, col] = part_up[...].astype(F32)
            down[:, col] = part_down[...].astype(F32)

    shape = jax.ShapeDtypeStruct((HALF, SIDE * w + extra), F32)
    spec = pl.BlockSpec((HALF, w), lambda i, here: (0, i))
    return line.call(
        body, SIDE, [partials] * (2 * n), half.grid_blocks(*up_from) + half.grid_blocks(*down_from),
        (shape, shape), (spec, spec),
    )


def send_far(line, half, partials):
    return send_part(line, half, partials, (2, 0), (2, 1), 0)


def send_raw(line, half, partials, extra):
    return send_part(line, half, partials, (1, 1), (-1, 0), extra)


def send_near(line, half, partials, far_up, far_down):
    w, n = half.width, half.count

    def body(here, *refs):
        far_up, far_down, up, down = refs[2 * n :]
        for col, (part_up, part_down) in tiles(n, *groups(refs[: 2 * n], n)):
            up[:, col] = part_up[...].astype(F32) + far_up[:, col]
            down[:, col] = part_down[...].astype(F32) + far_down[:, col]

    shape = jax.ShapeDtypeStruct((HALF, SIDE * w), F32)
    spec = pl.BlockSpec((HALF, w), lambda i, here: (0, i))
    return line.call(
        body, SIDE, [partials] * (2 * n) + [far_up, far_down],
        half.grid_blocks(1, 0) + half.grid_blocks(-1, 1) + [spec, spec],
        (shape, shape), (spec, spec),
    )


def repeat(arrays, n):
    return [array for array in arrays for _ in range(n)]


def high_low(part, raw_up, raw_down, near_up, near_down):
    high = part[:HALF].astype(F32) + near_up[...] + raw_down[...]
    low = part[HALF:].astype(F32) + near_down[...] + raw_up[...]
    return high, low


def send_far2(line, half, partials, got, into=None, first=0):
    w, n = half.width, half.count

    def body(here, *refs):
        up, down = refs[-2:]
        for col, blocks in tiles(n, *groups(refs[: 5 * n], n)):
            up[:, col], down[:, col] = high_low(*blocks)

    ins = [partials] * n + repeat(got, n)
    specs = half.one_blocks(2) + half.message_blocks(2) * 4
    shape = jax.ShapeDtypeStruct((HALF, w), F32)
    if into is None:
        return line.call(body, 1, ins, specs, (shape, shape), (whole(HALF, w), whole(HALF, w)))

    def by_tile(here, *refs):
        up, down = refs[-2:]
        for tile in range(n):

            @pl.when(pl.program_id(0) == tile)
            def _():
                up[...], down[...] = high_low(*(group[tile] for group in groups(refs[: 5 * n], n)))

    shape = jax.ShapeDtypeStruct(into[0].shape, F32)
    spec = pl.BlockSpec((HALF, TILE), lambda i, here: (0, first + i))
    return line.call(
        by_tile, n, ins + [*into], specs + [pl.BlockSpec(memory_space=pl.ANY)] * 2,
        (shape, shape), (spec, spec), aliases={len(ins) + 1: 0, len(ins) + 2: 1},
    )


def send_near2(line, half, partials, got, far, first=0):
    w, n = half.width, half.count

    def body(here, *refs):
        up, down = refs[-2:]
        for col, blocks in tiles(n, *groups(refs[: 12 * n], n)):
            high, low = high_low(*blocks[:5])
            up[:HALF, col] = high + blocks[10][...]
            up[HALF:, col] = low
            high, low = high_low(*blocks[5:10])
            down[:HALF, col] = high
            down[HALF:, col] = low + blocks[11][...]

    def far_spec(tile):
        return pl.BlockSpec((HALF, TILE), lambda i, here: (0, first + tile))

    shape = jax.ShapeDtypeStruct((BLOCK, w), F32)
    return line.call(
        body, 1,
        ([partials] * n + repeat(got, n)) * 2 + repeat(far, n),
        half.one_blocks(1) + half.message_blocks(1) * 4 + half.one_blocks(-1)
        + half.message_blocks(-1) * 4 + [far_spec(tile) for tile in range(n)] * 2,
        (shape, shape), (whole(BLOCK, w), whole(BLOCK, w)),
    )


def product(parts, value):
    high = value.astype(BF16)
    low = (value - high.astype(F32)).astype(BF16)
    return jnp.dot(
        parts[...], jnp.concatenate([high, low, high, low], axis=0), preferred_element_type=F32
    )


def finish(line, pair, partials, momentum, positions, got, tables, so_far):
    n = pair[0].count
    first = pair[0].first
    ins, specs = [], []
    for number, (half, arrays) in enumerate(zip(pair, got)):
        ins += [partials, *arrays]

        def tile(i, number=number):
            return jnp.minimum(i, n - 1) if number == 0 else jnp.maximum(i - n, 0)

        def part(i, here, half=half, tile=tile):
            return 0, half.column(here, 0, half.second(here, 0)) + tile(i)

        def message(i, here, half=half, tile=tile):
            return 0, half.second(here, 0) * n + tile(i)

        def flat(i, here, tile=tile):
            return 0, tile(i)

        specs += [pl.BlockSpec((BLOCK, TILE), part)]
        specs += [pl.BlockSpec((HALF, TILE), message)] * 4
        specs += [pl.BlockSpec((BLOCK, TILE), flat)] * 2
    along = lambda rows: pl.BlockSpec((1, rows, TILE), lambda i, here: (0, 0, first + i))
    ins += [momentum, positions, *tables]
    specs += [along(BLOCK), along(KEEP), whole(BLOCK, 4 * BLOCK), whole(BLOCK, 4 * BLOCK)]
    aliases = {}
    if so_far is not None:
        ins.append(so_far)
        specs.append(pl.BlockSpec(memory_space=pl.ANY))
        aliases = {len(ins): 0}

    def body(here, *refs):
        momentum, positions, forward, backward = refs[14:18]
        fresh, values = refs[-2:]
        freq = lax.broadcasted_iota(jnp.int32, (BLOCK, TILE), 0)

        def settle(part, raw_up, raw_down, near_up, near_down, left2, right2):
            grad = jnp.concatenate(high_low(part, raw_up, raw_down, near_up, near_down), axis=0)
            grad = grad + left2[...] + right2[...]
            moment = 0.9 * momentum[0] + grad
            coeff = product(forward, moment)
            chosen = positions[0]
            own = jnp.zeros_like(coeff)
            rows = []
            for place in range(KEEP):
                hit = jnp.where(chosen[place : place + 1] == freq, coeff, 0.0)
                rows.append(jnp.sum(hit, axis=0, keepdims=True))
                own = own + hit
            values[...] = jnp.concatenate(rows, axis=0)
            fresh[0] = moment - product(backward, own)

        @pl.when(pl.program_id(0) < n)
        def _():
            settle(*refs[0:7])

        @pl.when(pl.program_id(0) >= n)
        def _():
            settle(*refs[7:14])

    spans = 2 * n * TILE
    return line.call(
        body, 2 * n, ins, specs,
        (jax.ShapeDtypeStruct(momentum.shape, F32), jax.ShapeDtypeStruct((KEEP, spans), F32)),
        (along(BLOCK), pl.BlockSpec((KEEP, TILE), lambda i, here: (0, i))),
        aliases=aliases,
    )


def spread(line, first, lists, places, table):
    spans = lists[0].shape[1]

    def body(here, *refs):
        backward, out = refs[-2:]
        freq = lax.broadcasted_iota(jnp.int32, (BLOCK, TILE), 0)
        dense = []
        for values, chosen in zip(refs[:4], refs[4:8]):
            acc = jnp.zeros((BLOCK, TILE), F32)
            for place in range(KEEP):
                hit = chosen[0, place : place + 1] == freq
                acc = jnp.where(hit, values[place : place + 1], acc)
            dense.append(acc)
        out[...] = product(backward, (dense[0] + dense[3]) + (dense[1] + dense[2]))

    return line.call(
        body, spans // TILE, [*lists, *places, table],
        [pl.BlockSpec((KEEP, TILE), lambda i, here: (0, i))] * 4
        + [pl.BlockSpec((1, KEEP, TILE), lambda i, here: (0, 0, first + i))] * 4
        + [whole(BLOCK, 4 * BLOCK)],
        (jax.ShapeDtypeStruct((BLOCK, spans), F32),),
        (pl.BlockSpec((BLOCK, TILE), lambda i, here: (0, i)),),
    )[0]


def join(line, first, mine, other, spans, so_far):
    count = mine.shape[1] // TILE
    flat = pl.BlockSpec((BLOCK, TILE), lambda i, here: (0, i))
    ins, specs, aliases = [mine, other], [flat, flat], {}
    if so_far is not None:
        ins.append(so_far)
        specs.append(pl.BlockSpec(memory_space=pl.ANY))
        aliases = {3: 0}

    def body(here, *refs):
        refs[-1][...] = refs[0][...] + refs[1][...]

    return line.call(
        body, count, ins, specs, (jax.ShapeDtypeStruct((BLOCK, spans), F32),),
        (pl.BlockSpec((BLOCK, TILE), lambda i, here: (0, first + i)),),
        aliases=aliases,
    )[0]


def shift(dy, dx):
    return [
        (y * SIDE + x, (y + dy) % SIDE * SIDE + (x + dx) % SIDE)
        for y in range(SIDE)
        for x in range(SIDE)
    ]


def along(x_first, value, step):
    return lax.ppermute(value, "fsdp", shift(0, step) if x_first else shift(step, 0))


def along_z(value, step):
    return lax.ppermute(
        value, "rep", [(z * 2 + c, (z + step) % SIDE * 2 + c) for z in range(SIDE) for c in range(2)]
    )


def other_core(value):
    return lax.ppermute(value, "rep", [(r, r ^ 1) for r in range(2 * SIDE)])


def both(x_first, sent):
    return [along(x_first, sent[0], 1), along(x_first, sent[1], -1)]


def on_device(partials, momentum, positions):
    spans = momentum.shape[2]
    flat = partials.reshape(partials.shape[2:])
    me = lax.axis_index("fsdp")
    here = jnp.stack([me // SIDE, lax.rem(me, SIDE)]).astype(jnp.int32)
    tables = tuple(jnp.asarray(part) for part in dct_parts())
    line = Line(here)
    offset = dict.fromkeys(PIECES, 0)
    pairs = {
        name: (Half(True, start, width, spans), Half(False, start + width, width, spans))
        for name, (start, width) in PIECES.items()
    }
    places = [positions] + [along_z(positions, step) for step in (1, -1, 2)]
    got, sent = {}, []
    fresh = update = None
    for index, step in enumerate(ORDER.split()):
        name, stage, *guest = step
        pair = pairs[name]
        line.arrived = sent[index - 2] if index >= 2 else []
        before = lambda *stages, name=name: [
            [*sum((got[name, s][h] for s in stages), [])] for h in range(2)
        ]
        if stage == "1":
            out = [both(h.x_first, send_far(line, h, flat)) for h in pair]
        elif stage == "2" and not guest:
            out = [both(h.x_first, send_raw(line, h, flat, 0)) for h in pair]
        elif stage == "2":
            guests = pairs[guest[0]][::-1]
            out = []
            for half, other, g in zip(pair, guests, before(2, 3, name=guest[0])[::-1]):
                parts = send_raw(line, half, flat, other.width)
                parts = send_far2(line, other, flat, g, parts, SIDE * half.count)
                out.append(both(half.x_first, parts))
            got[guest[0], 4] = out[::-1]
            offset[guest[0]] = SIDE * pair[0].count
        elif stage == "3":
            out = [both(h.x_first, send_near(line, h, flat, *g)) for h, g in zip(pair, before(1))]
        elif stage == "4":
            out = [
                both(not h.x_first, send_far2(line, h, flat, g)) for h, g in zip(pair, before(2, 3))
            ]
        elif stage == "5":
            out = [
                both(not h.x_first, send_near2(line, h, flat, g, f, offset[name]))
                for h, g, f in zip(pair, before(2, 3), before(4))
            ]
        elif stage == "6":
            fresh, own = finish(
                line, pair, flat, momentum, positions, before(2, 3, 5), tables, fresh
            )
            lists = [own] + [along_z(own, step) for step in (1, -1, 2)]
            out = [lists[1:], lists]
        elif stage == "7":
            mine = spread(line, pair[0].first, got[name, 6][1], places, tables[1])
            out = [[other_core(mine)], [mine]]
        elif stage == "8":
            (other,), (mine,) = got[name, 7]
            update = join(line, pair[0].first, mine, other, spans, update)
            out = []
        got[name, int(stage)] = out
        sent.append(sum(out, []) if int(stage) < 6 else (out[0] if out else []))
        if step in PLACES_WITH:
            sent[-1] = sent[-1] + [places[1 + PLACES_WITH.index(step)]]
    return update, fresh


def solution(mesh):
    placed = (P("rep", "fsdp", None, None), P("rep", None, "fsdp"), P("rep", None, "fsdp"))
    return jax.shard_map(
        on_device,
        mesh=mesh,
        in_specs=placed,
        out_specs=(P(None, "fsdp"), P("rep", None, "fsdp")),
        check_vma=False,
    )
```

```python
import jax
import jax.numpy as jnp
import ml_dtypes
import numpy as np
from jax import lax
from jax.experimental import pallas as pl
from jax.experimental.pallas import tpu as pltpu
from jax.sharding import PartitionSpec as P

BLOCK = 64
HALF = BLOCK // 2
KEEP = 8
SIDE = 4
TILE = 512
WIDTH = 2048
CHUNKS = (2048, 2048)
EARLY = False
MOVED = 0
VMEM_LIMIT = 48 * 1024 * 1024
F32 = jnp.float32
BF16 = jnp.bfloat16


def dct_parts():
    k = np.arange(BLOCK, dtype=np.float64)[:, None]
    n = np.arange(BLOCK, dtype=np.float64)[None, :]
    scale = np.where(k == 0, np.sqrt(1.0 / BLOCK), np.sqrt(2.0 / BLOCK))
    dct = scale * np.cos(np.pi * (2.0 * n + 1.0) * k / (2.0 * BLOCK))

    def wide(mat):
        high = mat.astype(ml_dtypes.bfloat16)
        low = (mat - high.astype(np.float64)).astype(ml_dtypes.bfloat16)
        return np.concatenate([high, high, low, low], axis=1)

    return wide(dct), wide(dct.T.copy())


def fold(coord, step):
    return lax.rem(coord + (step + SIDE), SIDE)


class Half:
    def __init__(self, x_first, start, width, spans):
        self.x_first = x_first
        self.width = width
        self.count = width // TILE
        self.first = start // TILE
        self.per_target = spans // TILE

    def column(self, here, step, other):
        y, x = here[0], here[1]
        if self.x_first:
            target = other * SIDE + fold(x, step)
        else:
            target = fold(y, step) * SIDE + other
        return target * self.per_target + self.first

    def second(self, here, step):
        return fold(here[0] if self.x_first else here[1], step)

    def grid_blocks(self, step, rows):
        def spec(tile):
            return pl.BlockSpec(
                (HALF, TILE), lambda i, here: (rows, self.column(here, step, i) + tile)
            )

        return [spec(tile) for tile in range(self.count)]

    def one_blocks(self, step):
        def spec(tile):
            return pl.BlockSpec(
                (BLOCK, TILE),
                lambda i, here: (0, self.column(here, 0, self.second(here, step)) + tile),
            )

        return [spec(tile) for tile in range(self.count)]

    def message_blocks(self, step):
        def spec(tile):
            return pl.BlockSpec(
                (HALF, TILE), lambda i, here: (0, self.second(here, step) * self.count + tile)
            )

        return [spec(tile) for tile in range(self.count)]


def whole(*shape):
    return pl.BlockSpec(shape, lambda i, here: (0,) * len(shape))


class Line:
    def __init__(self, here):
        self.here = here
        self.token = None
        self.arrived = []

    def call(self, body, grid, ins, in_specs, out_shape, out_specs, aliases=None):
        ins, in_specs = list(ins), list(in_specs)
        count = len(ins)
        order = ([] if self.token is None else [self.token]) + self.arrived
        taken = len(order)
        ins += order
        in_specs += [whole(*(1,) * (array.ndim - 2), 8, 128) for array in order]

        def run(here, *refs):
            refs[-1][...] = jnp.zeros((8, 128), F32)
            body(here, *refs[:count], *refs[count + taken : -1])

        *outs, self.token = pl.pallas_call(
            run,
            grid_spec=pltpu.PrefetchScalarGridSpec(
                num_scalar_prefetch=1,
                grid=(grid,),
                in_specs=in_specs,
                out_specs=(*out_specs, whole(8, 128)),
            ),
            out_shape=(*out_shape, jax.ShapeDtypeStruct((8, 128), F32)),
            input_output_aliases=aliases or {},
            compiler_params=pltpu.CompilerParams(vmem_limit_bytes=VMEM_LIMIT),
            cost_estimate=pl.CostEstimate(flops=0, bytes_accessed=MOVED, transcendentals=0),
        )(self.here, *ins)
        return outs


def tiles(n, *groups):
    for tile in range(n):
        yield slice(tile * TILE, (tile + 1) * TILE), [group[tile] for group in groups]


def groups(refs, n):
    return [refs[k : k + n] for k in range(0, len(refs), n)]


def send_part(line, half, partials, up_from, down_from):
    w, n = half.width, half.count

    def body(here, *refs):
        up, down = refs[2 * n :]
        for col, (part_up, part_down) in tiles(n, *groups(refs[: 2 * n], n)):
            up[:, col] = part_up[...].astype(F32)
            down[:, col] = part_down[...].astype(F32)

    shape = jax.ShapeDtypeStruct((HALF, SIDE * w), F32)
    spec = pl.BlockSpec((HALF, w), lambda i, here: (0, i))
    return line.call(
        body, SIDE, [partials] * (2 * n), half.grid_blocks(*up_from) + half.grid_blocks(*down_from),
        (shape, shape), (spec, spec),
    )


def send_far(line, half, partials):
    return send_part(line, half, partials, (2, 0), (2, 1))


def send_raw(line, half, partials):
    return send_part(line, half, partials, (1, 1), (-1, 0))


def send_near(line, half, partials, far_up, far_down):
    w, n = half.width, half.count

    def body(here, *refs):
        far_up, far_down, up, down = refs[2 * n :]
        for col, (part_up, part_down) in tiles(n, *groups(refs[: 2 * n], n)):
            up[:, col] = part_up[...].astype(F32) + far_up[:, col]
            down[:, col] = part_down[...].astype(F32) + far_down[:, col]

    shape = jax.ShapeDtypeStruct((HALF, SIDE * w), F32)
    spec = pl.BlockSpec((HALF, w), lambda i, here: (0, i))
    return line.call(
        body, SIDE, [partials] * (2 * n) + [far_up, far_down],
        half.grid_blocks(1, 0) + half.grid_blocks(-1, 1) + [spec, spec],
        (shape, shape), (spec, spec),
    )


def repeat(arrays, n):
    return [array for array in arrays for _ in range(n)]


def high_low(part, raw_up, raw_down, near_up, near_down):
    high = part[:HALF].astype(F32) + near_up[...] + raw_down[...]
    low = part[HALF:].astype(F32) + near_down[...] + raw_up[...]
    return high, low


def send_far2(line, half, partials, got):
    w, n = half.width, half.count

    def body(here, *refs):
        up, down = refs[-2:]
        for col, blocks in tiles(n, *groups(refs[: 5 * n], n)):
            up[:, col], down[:, col] = high_low(*blocks)

    shape = jax.ShapeDtypeStruct((HALF, w), F32)
    return line.call(
        body, 1, [partials] * n + repeat(got, n), half.one_blocks(2) + half.message_blocks(2) * 4,
        (shape, shape), (whole(HALF, w), whole(HALF, w)),
    )


def send_near2(line, half, partials, got, far):
    w, n = half.width, half.count

    def body(here, *refs):
        up, down = refs[-2:]
        for col, blocks in tiles(n, *groups(refs[: 12 * n], n)):
            high, low = high_low(*blocks[:5])
            up[:HALF, col] = high + blocks[10][...]
            up[HALF:, col] = low
            high, low = high_low(*blocks[5:10])
            down[:HALF, col] = high
            down[HALF:, col] = low + blocks[11][...]

    def far_spec(tile):
        return pl.BlockSpec((HALF, TILE), lambda i, here: (0, tile))

    shape = jax.ShapeDtypeStruct((BLOCK, w), F32)
    return line.call(
        body, 1,
        ([partials] * n + repeat(got, n)) * 2 + repeat(far, n),
        half.one_blocks(1) + half.message_blocks(1) * 4 + half.one_blocks(-1)
        + half.message_blocks(-1) * 4 + [far_spec(tile) for tile in range(n)] * 2,
        (shape, shape), (whole(BLOCK, w), whole(BLOCK, w)),
    )


def product(parts, value):
    high = value.astype(BF16)
    low = (value - high.astype(F32)).astype(BF16)
    return jnp.dot(
        parts[...], jnp.concatenate([high, low, high, low], axis=0), preferred_element_type=F32
    )


def settle(grad, momentum, positions, forward, backward, fresh, values):
    freq = lax.broadcasted_iota(jnp.int32, grad.shape, 0)
    moment = 0.9 * momentum[0] + grad
    coeff = product(forward, moment)
    chosen = positions[0]
    own = jnp.zeros_like(coeff)
    rows = []
    for place in range(KEEP):
        hit = jnp.where(chosen[place : place + 1] == freq, coeff, 0.0)
        rows.append(jnp.sum(hit, axis=0, keepdims=True))
        own = own + hit
    values[...] = jnp.concatenate(rows, axis=0)
    fresh[0] = moment - product(backward, own)


def finish(line, pair, partials, momentum, positions, got, tables, so_far):
    n = pair[0].count
    first = pair[0].first
    ins, specs = [], []
    for number, (half, arrays) in enumerate(zip(pair, got)):
        ins += [partials, *arrays]

        def tile(i, number=number):
            return jnp.minimum(i, n - 1) if number == 0 else jnp.maximum(i - n, 0)

        def part(i, here, half=half, tile=tile):
            return 0, half.column(here, 0, half.second(here, 0)) + tile(i)

        def message(i, here, half=half, tile=tile):
            return 0, half.second(here, 0) * n + tile(i)

        def flat(i, here, tile=tile):
            return 0, tile(i)

        specs += [pl.BlockSpec((BLOCK, TILE), part)]
        specs += [pl.BlockSpec((HALF, TILE), message)] * 4
        specs += [pl.BlockSpec((BLOCK, TILE), flat)] * 2
    along = lambda rows: pl.BlockSpec((1, rows, TILE), lambda i, here: (0, 0, first + i))
    ins += [momentum, positions, *tables]
    specs += [along(BLOCK), along(KEEP), whole(BLOCK, 4 * BLOCK), whole(BLOCK, 4 * BLOCK)]
    aliases = {}
    if so_far is not None:
        ins.append(so_far)
        specs.append(pl.BlockSpec(memory_space=pl.ANY))
        aliases = {len(ins): 0}

    def body(here, *refs):
        momentum, positions, forward, backward = refs[14:18]

        def half(part, raw_up, raw_down, near_up, near_down, left2, right2):
            grad = jnp.concatenate(high_low(part, raw_up, raw_down, near_up, near_down), axis=0)
            grad = grad + left2[...] + right2[...]
            settle(grad, momentum, positions, forward, backward, *refs[-2:])

        @pl.when(pl.program_id(0) < n)
        def _():
            half(*refs[0:7])

        @pl.when(pl.program_id(0) >= n)
        def _():
            half(*refs[7:14])

    spans = 2 * n * TILE
    return line.call(
        body, 2 * n, ins, specs,
        (jax.ShapeDtypeStruct(momentum.shape, F32), jax.ShapeDtypeStruct((KEEP, spans), F32)),
        (along(BLOCK), pl.BlockSpec((KEEP, TILE), lambda i, here: (0, i))),
        aliases=aliases,
    )


def widen(line, start, width, spans, partials):
    n = width // TILE

    def body(here, *refs):
        for col, (part,) in tiles(n, refs[:n]):
            refs[n][0, :, col] = part[...].astype(F32)

    def spec(tile):
        return pl.BlockSpec(
            (BLOCK, TILE), lambda i, here: (0, i * (spans // TILE) + start // TILE + tile)
        )

    targets = SIDE * SIDE
    return line.call(
        body, targets, [partials] * n, [spec(tile) for tile in range(n)],
        (jax.ShapeDtypeStruct((targets, BLOCK, width), F32),),
        (pl.BlockSpec((1, BLOCK, width), lambda i, here: (i, 0, 0)),),
    )[0]


def finish_sum(line, summed, offset, start, width, momentum, positions, tables, so_far):
    along = lambda rows: pl.BlockSpec((1, rows, TILE), lambda i, here: (0, 0, start // TILE + i))

    def body(here, summed, momentum, positions, forward, backward, so_far, fresh, values):
        settle(summed[...], momentum, positions, forward, backward, fresh, values)

    return line.call(
        body, width // TILE, [summed, momentum, positions, *tables, so_far],
        [pl.BlockSpec((BLOCK, TILE), lambda i, here: (0, offset // TILE + i)), along(BLOCK),
         along(KEEP), whole(BLOCK, 4 * BLOCK), whole(BLOCK, 4 * BLOCK),
         pl.BlockSpec(memory_space=pl.ANY)],
        (jax.ShapeDtypeStruct(momentum.shape, F32), jax.ShapeDtypeStruct((KEEP, width), F32)),
        (along(BLOCK), pl.BlockSpec((KEEP, TILE), lambda i, here: (0, i))), aliases={6: 0},
    )


def dense(values, chosen):
    freq = lax.broadcasted_iota(jnp.int32, (BLOCK, values.shape[1]), 0)
    acc = jnp.zeros((BLOCK, values.shape[1]), F32)
    for place in range(KEEP):
        acc = jnp.where(chosen[place : place + 1] == freq, values[place : place + 1], acc)
    return acc


def spread_all(line, start, values, places, table, spans):
    reps, _, width = values.shape

    def body(here, values, chosen, backward, out):
        total = dense(values[0], chosen[0])
        for rep in range(1, reps):
            total = total + dense(values[rep], chosen[rep])
        out[...] = product(backward, total)

    return line.call(
        body, width // TILE, [values, places, table],
        [pl.BlockSpec((reps, KEEP, TILE), lambda i, here: (0, 0, i)),
         pl.BlockSpec((reps, KEEP, TILE), lambda i, here: (0, 0, start // TILE + i)),
         whole(BLOCK, 4 * BLOCK)],
        (jax.ShapeDtypeStruct((BLOCK, spans), F32),),
        (pl.BlockSpec((BLOCK, TILE), lambda i, here: (0, start // TILE + i)),),
    )[0]


def spread(line, start, lists, places, table):
    width = lists[0].shape[1]

    def body(here, *refs):
        backward, out = refs[-2:]
        parts = [dense(refs[k][...], refs[4 + k][0]) for k in range(4)]
        out[...] = product(backward, (parts[0] + parts[3]) + (parts[1] + parts[2]))

    def of(step):
        return pl.BlockSpec(
            (1, KEEP, TILE),
            lambda i, here: (fold(here[2], step) * 2 + here[3], 0, start // TILE + i),
        )

    return line.call(
        body, width // TILE, [*lists, *[places] * 4, table],
        [pl.BlockSpec((KEEP, TILE), lambda i, here: (0, i))] * 4
        + [of(step) for step in (0, -1, 1, 2)] + [whole(BLOCK, 4 * BLOCK)],
        (jax.ShapeDtypeStruct((BLOCK, width), F32),),
        (pl.BlockSpec((BLOCK, TILE), lambda i, here: (0, i)),),
    )[0]


def join(line, start, mine, other, so_far):
    flat = pl.BlockSpec((BLOCK, TILE), lambda i, here: (0, i))

    def body(here, mine, other, so_far, out):
        out[...] = mine[...] + other[...]

    return line.call(
        body, mine.shape[1] // TILE, [mine, other, so_far],
        [flat, flat, pl.BlockSpec(memory_space=pl.ANY)],
        (jax.ShapeDtypeStruct(so_far.shape, F32),),
        (pl.BlockSpec((BLOCK, TILE), lambda i, here: (0, start // TILE + i)),), aliases={3: 0},
    )[0]


def shift(dy, dx):
    return [
        (y * SIDE + x, (y + dy) % SIDE * SIDE + (x + dx) % SIDE)
        for y in range(SIDE)
        for x in range(SIDE)
    ]


def along(x_first, value, step):
    return lax.ppermute(value, "fsdp", shift(0, step) if x_first else shift(step, 0))


def along_z(value, step):
    return lax.ppermute(
        value, "rep", [(z * 2 + c, (z + step) % SIDE * 2 + c) for z in range(SIDE) for c in range(2)]
    )


def other_core(value):
    return lax.ppermute(value, "rep", [(r, r ^ 1) for r in range(2 * SIDE)])


def both(x_first, sent):
    return [along(x_first, sent[0], 1), along(x_first, sent[1], -1)]


def on_device(partials, momentum, positions):
    spans = momentum.shape[2]
    flat = partials.reshape(partials.shape[2:])
    me, rep = lax.axis_index("fsdp"), lax.axis_index("rep")
    here = jnp.stack([me // SIDE, lax.rem(me, SIDE), rep // 2, lax.rem(rep, 2)]).astype(jnp.int32)
    tables = tuple(jnp.asarray(part) for part in dct_parts())
    line = Line(here)
    pair = (Half(True, 0, WIDTH, spans), Half(False, WIDTH, WIDTH, spans))
    start = 2 * WIDTH
    got, sent = {}, []

    def each(stage, send):
        out = [None, None]
        for axis in range(2):
            h = axis if stage < 4 else 1 - axis
            line.arrived = sent[-2][axis] if len(sent) >= 2 else []
            out[h] = both(axis == 0, send(pair[h], h))
        line.arrived = []
        got[stage] = out
        sent.append(out if stage < 4 else out[::-1])

    def before(h, *stages):
        return sum((got[stage][h] for stage in stages), [])

    places = lax.all_gather(positions[0], "rep", axis=0, tiled=False)
    each(1, lambda half, h: send_far(line, half, flat))
    wide = widen(line, start, spans - start, spans, flat)
    summed = lax.psum_scatter(wide, "fsdp", scatter_dimension=0, tiled=False)
    each(2, lambda half, h: send_raw(line, half, flat))
    each(3, lambda half, h: send_near(line, half, flat, *before(h, 1)))
    each(4, lambda half, h: send_far2(line, half, flat, before(h, 2, 3)))
    each(5, lambda half, h: send_near2(line, half, flat, before(h, 2, 3), before(h, 4)))
    full = [before(h, 2, 3, 5) for h in range(2)]
    fresh, own = finish(line, pair, flat, momentum, positions, full, tables, None)
    every = lax.all_gather(own, "rep", axis=0, tiled=False)
    if EARLY:
        update = spread_all(line, 0, every, places, tables[1], spans)
    lists, offset = [], 0
    for width in CHUNKS:
        fresh, own = finish_sum(
            line, summed, offset, start + offset, width, momentum, positions, tables, fresh
        )
        lists.append([own] + [along_z(own, step) for step in (1, -1, 2)])
        offset += width
    if not EARLY:
        update = spread_all(line, 0, every, places, tables[1], spans)
    mine, offset = [], 0
    for width, four in zip(CHUNKS, lists):
        mine.append(spread(line, start + offset, four, places, tables[1]))
        offset += width
    offset = 0
    for width, part in zip(CHUNKS, mine):
        update = join(line, start + offset, part, other_core(part), update)
        offset += width
    return update, fresh


def solution(mesh):
    placed = (P("rep", "fsdp", None, None), P("rep", None, "fsdp"), P("rep", None, "fsdp"))
    return jax.shard_map(
        on_device,
        mesh=mesh,
        in_specs=placed,
        out_specs=(P(None, "fsdp"), P("rep", None, "fsdp")),
        check_vma=False,
    )
```

```python
import jax
import jax.numpy as jnp
import ml_dtypes
import numpy as np
from jax import lax
from jax.experimental import pallas as pl
from jax.experimental.pallas import tpu as pltpu
from jax.sharding import PartitionSpec as P

BLOCK = 64
HALF = BLOCK // 2
KEEP = 8
SIDE = 4
TILE = 1024
CHUNK = 256
PARTS = (2, 2)
TILE = 1024
CHUNK = 256
WIDTH = 2048
CHUNKS = (2048, 2048)
VMEM_LIMIT = 48 * 1024 * 1024
F32 = jnp.float32
BF16 = jnp.bfloat16


def dct_parts():
    k = np.arange(BLOCK, dtype=np.float64)[:, None]
    n = np.arange(BLOCK, dtype=np.float64)[None, :]
    scale = np.where(k == 0, np.sqrt(1.0 / BLOCK), np.sqrt(2.0 / BLOCK))
    dct = scale * np.cos(np.pi * (2.0 * n + 1.0) * k / (2.0 * BLOCK))

    def wide(mat):
        high = mat.astype(ml_dtypes.bfloat16)
        low = (mat - high.astype(np.float64)).astype(ml_dtypes.bfloat16)
        return np.concatenate([high, high, low, low], axis=1)

    return wide(dct), wide(dct.T.copy())


def fold(coord, step):
    return lax.rem(coord + (step + SIDE), SIDE)


class Half:
    def __init__(self, x_first, start, width, spans):
        self.x_first = x_first
        self.width = width
        self.count = width // TILE
        self.first = start // TILE
        self.per_target = spans // TILE

    def column(self, here, step, other):
        y, x = here[0], here[1]
        if self.x_first:
            target = other * SIDE + fold(x, step)
        else:
            target = fold(y, step) * SIDE + other
        return target * self.per_target + self.first

    def second(self, here, step):
        return fold(here[0] if self.x_first else here[1], step)

    def grid_blocks(self, step, rows):
        def spec(tile):
            return pl.BlockSpec(
                (HALF, TILE), lambda i, here: (rows, self.column(here, step, i) + tile)
            )

        return [spec(tile) for tile in range(self.count)]

    def one_blocks(self, step):
        def spec(tile):
            return pl.BlockSpec(
                (BLOCK, TILE),
                lambda i, here: (0, self.column(here, 0, self.second(here, step)) + tile),
            )

        return [spec(tile) for tile in range(self.count)]

    def message_blocks(self, step):
        def spec(tile):
            return pl.BlockSpec(
                (HALF, TILE), lambda i, here: (0, self.second(here, step) * self.count + tile)
            )

        return [spec(tile) for tile in range(self.count)]


def whole(*shape):
    return pl.BlockSpec(shape, lambda i, here: (0,) * len(shape))


class Line:
    def __init__(self, here):
        self.here = here
        self.token = None
        self.arrived = []

    def call(self, body, grid, ins, in_specs, out_shape, out_specs, aliases=None):
        ins, in_specs = list(ins), list(in_specs)
        count = len(ins)
        order = ([] if self.token is None else [self.token]) + self.arrived
        taken = len(order)
        ins += order
        in_specs += [whole(*(1,) * (array.ndim - 2), 8, 128) for array in order]

        def run(here, *refs):
            refs[-1][...] = jnp.zeros((8, 128), F32)
            body(here, *refs[:count], *refs[count + taken : -1])

        *outs, self.token = pl.pallas_call(
            run,
            grid_spec=pltpu.PrefetchScalarGridSpec(
                num_scalar_prefetch=1,
                grid=(grid,),
                in_specs=in_specs,
                out_specs=(*out_specs, whole(8, 128)),
            ),
            out_shape=(*out_shape, jax.ShapeDtypeStruct((8, 128), F32)),
            input_output_aliases=aliases or {},
            compiler_params=pltpu.CompilerParams(vmem_limit_bytes=VMEM_LIMIT),
            cost_estimate=pl.CostEstimate(flops=0, bytes_accessed=0, transcendentals=0),
        )(self.here, *ins)
        return outs


def tiles(n, *groups):
    for tile in range(n):
        yield slice(tile * TILE, (tile + 1) * TILE), [group[tile] for group in groups]


def groups(refs, n):
    return [refs[k : k + n] for k in range(0, len(refs), n)]


def send_part(line, half, partials, up_from, down_from):
    w, n = half.width, half.count

    def body(here, *refs):
        up, down = refs[2 * n :]
        for col, (part_up, part_down) in tiles(n, *groups(refs[: 2 * n], n)):
            up[:, col] = part_up[...].astype(F32)
            down[:, col] = part_down[...].astype(F32)

    shape = jax.ShapeDtypeStruct((HALF, SIDE * w), F32)
    spec = pl.BlockSpec((HALF, w), lambda i, here: (0, i))
    return line.call(
        body, SIDE, [partials] * (2 * n), half.grid_blocks(*up_from) + half.grid_blocks(*down_from),
        (shape, shape), (spec, spec),
    )


def send_far(line, half, partials):
    return send_part(line, half, partials, (2, 0), (2, 1))


def send_raw(line, half, partials):
    return send_part(line, half, partials, (1, 1), (-1, 0))


def send_near(line, half, partials, far_up, far_down):
    w, n = half.width, half.count

    def body(here, *refs):
        far_up, far_down, up, down = refs[2 * n :]
        for col, (part_up, part_down) in tiles(n, *groups(refs[: 2 * n], n)):
            up[:, col] = part_up[...].astype(F32) + far_up[:, col]
            down[:, col] = part_down[...].astype(F32) + far_down[:, col]

    shape = jax.ShapeDtypeStruct((HALF, SIDE * w), F32)
    spec = pl.BlockSpec((HALF, w), lambda i, here: (0, i))
    return line.call(
        body, SIDE, [partials] * (2 * n) + [far_up, far_down],
        half.grid_blocks(1, 0) + half.grid_blocks(-1, 1) + [spec, spec],
        (shape, shape), (spec, spec),
    )


def repeat(arrays, n):
    return [array for array in arrays for _ in range(n)]


def high_low(part, raw_up, raw_down, near_up, near_down):
    high = part[:HALF].astype(F32) + near_up[...] + raw_down[...]
    low = part[HALF:].astype(F32) + near_down[...] + raw_up[...]
    return high, low


def send_far2(line, half, partials, got):
    w, n = half.width, half.count

    def body(here, *refs):
        up, down = refs[-2:]
        for col, blocks in tiles(n, *groups(refs[: 5 * n], n)):
            up[:, col], down[:, col] = high_low(*blocks)

    shape = jax.ShapeDtypeStruct((HALF, w), F32)
    return line.call(
        body, 1, [partials] * n + repeat(got, n), half.one_blocks(2) + half.message_blocks(2) * 4,
        (shape, shape), (whole(HALF, w), whole(HALF, w)),
    )


def send_near2(line, half, partials, got, far, first, n):
    own = slice(first, first + n)

    def body(here, *refs):
        up, down = refs[-2:]
        for col, blocks in tiles(n, *groups(refs[: 12 * n], n)):
            high, low = high_low(*blocks[:5])
            up[:HALF, col] = high + blocks[10][...]
            up[HALF:, col] = low
            high, low = high_low(*blocks[5:10])
            down[:HALF, col] = high
            down[HALF:, col] = low + blocks[11][...]

    far_specs = [pl.BlockSpec((HALF, TILE), lambda i, here, t=t: (0, t)) for t in range(half.count)]
    w = n * TILE
    shape = jax.ShapeDtypeStruct((BLOCK, w), F32)
    return line.call(
        body, 1, ([partials] * n + repeat(got, n)) * 2 + repeat(far, n),
        half.one_blocks(1)[own] + half.message_blocks(1)[own] * 4 + half.one_blocks(-1)[own]
        + half.message_blocks(-1)[own] * 4 + far_specs[own] * 2,
        (shape, shape), (whole(BLOCK, w), whole(BLOCK, w)),
    )


def product(parts, value):
    high = value.astype(BF16)
    low = (value - high.astype(F32)).astype(BF16)
    return jnp.dot(
        parts[...], jnp.concatenate([high, low, high, low], axis=0), preferred_element_type=F32
    )


def settle(grad_of, momentum, positions, forward, backward, fresh, values):
    for at in range(0, TILE, CHUNK):
        col = slice(at, at + CHUNK)
        moment = 0.9 * momentum[0, :, col] + grad_of(col)
        coeff = product(forward, moment)
        chosen = positions[0, :, col]
        freq = lax.broadcasted_iota(jnp.int32, coeff.shape, 0)
        own = jnp.zeros_like(coeff)
        rows = []
        for place in range(KEEP):
            hit = jnp.where(chosen[place : place + 1] == freq, coeff, 0.0)
            rows.append(jnp.sum(hit, axis=0, keepdims=True))
            own = own + hit
        values[:, col] = jnp.concatenate(rows, axis=0)
        fresh[0, :, col] = moment - product(backward, own)


class Part:
    def __init__(self, pair, first, n):
        self.pair, self.first, self.n = pair, first, n
        self.steps, self.spans = 2 * n, 2 * n * TILE

    def place(self, i):
        return jnp.where(i < self.n, i, i - self.n + self.pair[0].count) + self.first

    def columns(self, rows):
        return pl.BlockSpec((1, rows, TILE), lambda i, here: (0, 0, self.place(i)))

    def result(self):
        return pl.BlockSpec((BLOCK, TILE), lambda i, here: (0, self.place(i)))

    def compact(self, rows):
        return pl.BlockSpec((rows, TILE), lambda i, here: (0, i))


def finish(line, piece, partials, momentum, positions, got, tables, so_far):
    n = piece.n
    ins, specs = [], []
    for number, (half, arrays) in enumerate(zip(piece.pair, got)):
        ins += [partials, *arrays]

        def tile(i, number=number):
            return jnp.minimum(i, n - 1) if number == 0 else jnp.maximum(i - n, 0)

        def part(i, here, half=half, tile=tile):
            return 0, half.column(here, 0, half.second(here, 0)) + piece.first + tile(i)

        def message(i, here, half=half, tile=tile):
            return 0, half.second(here, 0) * half.count + piece.first + tile(i)

        def flat(i, here, tile=tile):
            return 0, tile(i)

        specs += [pl.BlockSpec((BLOCK, TILE), part)]
        specs += [pl.BlockSpec((HALF, TILE), message)] * 4
        specs += [pl.BlockSpec((BLOCK, TILE), flat)] * 2
    ins += [momentum, positions, *tables]
    specs += [piece.columns(BLOCK), piece.columns(KEEP)] + [whole(BLOCK, 4 * BLOCK)] * 2
    aliases = {}
    if so_far is not None:
        ins.append(so_far)
        specs.append(pl.BlockSpec(memory_space=pl.ANY))
        aliases = {len(ins): 0}

    def body(here, *refs):
        momentum, positions, forward, backward = refs[14:18]

        def half(part, raw_up, raw_down, near_up, near_down, left2, right2):
            def grad_of(col):
                first = (raw_up, raw_down, near_up, near_down)
                pair = high_low(part[:, col], *(ref[:, col] for ref in first))
                return jnp.concatenate(pair, axis=0) + left2[:, col] + right2[:, col]

            settle(grad_of, momentum, positions, forward, backward, *refs[-2:])

        @pl.when(pl.program_id(0) < n)
        def _():
            half(*refs[0:7])

        @pl.when(pl.program_id(0) >= n)
        def _():
            half(*refs[7:14])

    return line.call(
        body, piece.steps, ins, specs,
        (jax.ShapeDtypeStruct(momentum.shape, F32), jax.ShapeDtypeStruct((KEEP, piece.spans), F32)),
        (piece.columns(BLOCK), piece.compact(KEEP)), aliases=aliases,
    )


def dense(values, chosen):
    freq = lax.broadcasted_iota(jnp.int32, (BLOCK, values.shape[1]), 0)
    acc = jnp.zeros((BLOCK, values.shape[1]), F32)
    for place in range(KEEP):
        acc = jnp.where(chosen[place : place + 1] == freq, values[place : place + 1], acc)
    return acc


def spread(line, piece, lists, places, table):
    def body(here, *refs):
        backward, out = refs[-2:]
        for at in range(0, TILE, CHUNK):
            col = slice(at, at + CHUNK)
            parts = [dense(refs[k][:, col], refs[4 + k][0, :, col]) for k in range(4)]
            out[:, col] = product(backward, (parts[0] + parts[3]) + (parts[1] + parts[2]))

    return line.call(
        body, piece.steps, [*lists, *places, table],
        [piece.compact(KEEP)] * 4 + [piece.columns(KEEP)] * 4 + [whole(BLOCK, 4 * BLOCK)],
        (jax.ShapeDtypeStruct((BLOCK, piece.spans), F32),), (piece.compact(BLOCK),),
    )[0]


def join(line, piece, mine, other, spans, so_far):
    ins, specs, aliases = [mine, other], [piece.compact(BLOCK)] * 2, {}
    if so_far is not None:
        ins.append(so_far)
        specs.append(pl.BlockSpec(memory_space=pl.ANY))
        aliases = {3: 0}

    def body(here, *refs):
        refs[-1][...] = refs[0][...] + refs[1][...]

    return line.call(
        body, piece.steps, ins, specs, (jax.ShapeDtypeStruct((BLOCK, spans), F32),),
        (piece.result(),), aliases=aliases,
    )[0]


def shift(dy, dx):
    return [
        (y * SIDE + x, (y + dy) % SIDE * SIDE + (x + dx) % SIDE)
        for y in range(SIDE)
        for x in range(SIDE)
    ]


def along(x_first, value, step):
    return lax.ppermute(value, "fsdp", shift(0, step) if x_first else shift(step, 0))


def along_z(value, step):
    return lax.ppermute(
        value, "rep", [(z * 2 + c, (z + step) % SIDE * 2 + c) for z in range(SIDE) for c in range(2)]
    )


def other_core(value):
    return lax.ppermute(value, "rep", [(r, r ^ 1) for r in range(2 * SIDE)])


def both(x_first, sent):
    return [along(x_first, sent[0], 1), along(x_first, sent[1], -1)]


def on_device(partials, momentum, positions):
    spans = momentum.shape[2]
    flat = partials.reshape(partials.shape[2:])
    me = lax.axis_index("fsdp")
    here = jnp.stack([me // SIDE, lax.rem(me, SIDE)]).astype(jnp.int32)
    tables = tuple(jnp.asarray(part) for part in dct_parts())
    line = Line(here)
    width = spans // 2
    pair = (Half(True, 0, width, spans), Half(False, width, width, spans))
    pieces, first = [], 0
    for n in PARTS:
        pieces.append(Part(pair, first, n))
        first += n
    got, sent = {}, []

    def each(stage, second, send):
        out = [None, None]
        for axis in range(2):
            h = 1 - axis if second else axis
            line.arrived = sent[-2][axis] if len(sent) >= 2 else []
            out[h] = both(axis == 0, send(pair[h], h))
        line.arrived = []
        got[stage] = out
        sent.append(out[::-1] if second else out)

    def before(h, *stages):
        return sum((got[stage][h] for stage in stages), [])

    places = [positions] + [along_z(positions, step) for step in (1, -1, 2)]
    each("far", False, lambda half, h: send_far(line, half, flat))
    each("raw", False, lambda half, h: send_raw(line, half, flat))
    sent[0] = [sent[0][0], sent[0][1] + places[1:2]]
    each("near", False, lambda half, h: send_near(line, half, flat, *before(h, "far")))
    sent[1] = [sent[1][0], sent[1][1] + places[2:]]
    each("far2", True, lambda half, h: send_far2(line, half, flat, before(h, "raw", "near")))
    for number, piece in enumerate(pieces):
        each(
            number, True,
            lambda half, h: send_near2(
                line, half, flat, before(h, "raw", "near"), before(h, "far2"), piece.first, piece.n
            ),
        )
    fresh = update = None
    lists, mine = [], []
    for number, piece in enumerate(pieces):
        full = [before(h, "raw", "near", number) for h in range(2)]
        fresh, own = finish(line, piece, flat, momentum, positions, full, tables, fresh)
        lists.append([own] + [along_z(own, step) for step in (1, -1, 2)])
    for piece, four in zip(pieces, lists):
        mine.append(spread(line, piece, four, places, tables[1]))
    for piece, part in zip(pieces, mine):
        update = join(line, piece, part, other_core(part), spans, update)
    return update, fresh


def solution(mesh):
    placed = (P("rep", "fsdp", None, None), P("rep", None, "fsdp"), P("rep", None, "fsdp"))
    return jax.shard_map(
        on_device,
        mesh=mesh,
        in_specs=placed,
        out_specs=(P(None, "fsdp"), P("rep", None, "fsdp")),
        check_vma=False,
    )
```

```python
import jax
import jax.numpy as jnp
import ml_dtypes
import numpy as np
from jax import lax
from jax.experimental import pallas as pl
from jax.experimental.pallas import tpu as pltpu
from jax.sharding import PartitionSpec as P

BLOCK = 64
HALF = BLOCK // 2
KEEP = 8
SIDE = 4
TILE = 1024
CHUNK = 256
FINE, BROAD = 512, 1024
PARTS = (2, 2)
AXES = (0, 0, 1, 1, 1, 1)
LAG = (2, 2, 2, 2, 2, 2)
PLACES_WITH = ((1, 0), (1, 0), (1, 1))
STEPS = (1, -1, 2)
TAIL = ("f0", "f1", "s0", "j0", "s1", "j1")
VMEM_LIMIT = 40 * 1024 * 1024
F32 = jnp.float32
BF16 = jnp.bfloat16


def dct_parts():
    k = np.arange(BLOCK, dtype=np.float64)[:, None]
    n = np.arange(BLOCK, dtype=np.float64)[None, :]
    scale = np.where(k == 0, np.sqrt(1.0 / BLOCK), np.sqrt(2.0 / BLOCK))
    dct = scale * np.cos(np.pi * (2.0 * n + 1.0) * k / (2.0 * BLOCK))

    def wide(mat):
        high = mat.astype(ml_dtypes.bfloat16)
        low = (mat - high.astype(np.float64)).astype(ml_dtypes.bfloat16)
        return np.concatenate([high, high, low, low], axis=1)

    return wide(dct), wide(dct.T.copy())


def fold(coord, step):
    return lax.rem(coord + (step + SIDE), SIDE)


class Half:
    def __init__(self, x_first, start, width, spans):
        self.x_first = x_first
        self.width = width
        self.count = width // TILE
        self.first = start // TILE
        self.per_target = spans // TILE

    def column(self, here, step, other):
        y, x = here[0], here[1]
        if self.x_first:
            target = other * SIDE + fold(x, step)
        else:
            target = fold(y, step) * SIDE + other
        return target * self.per_target + self.first

    def second(self, here, step):
        return fold(here[0] if self.x_first else here[1], step)

    def grid_blocks(self, step, rows):
        def spec(tile):
            return pl.BlockSpec(
                (HALF, TILE), lambda i, here: (rows, self.column(here, step, i) + tile)
            )

        return [spec(tile) for tile in range(self.count)]

    def one_blocks(self, step):
        def spec(tile):
            return pl.BlockSpec(
                (BLOCK, TILE),
                lambda i, here: (0, self.column(here, 0, self.second(here, step)) + tile),
            )

        return [spec(tile) for tile in range(self.count)]

    def message_blocks(self, step):
        def spec(tile):
            return pl.BlockSpec(
                (HALF, TILE), lambda i, here: (0, self.second(here, step) * self.count + tile)
            )

        return [spec(tile) for tile in range(self.count)]


def whole(*shape):
    return pl.BlockSpec(shape, lambda i, here: (0,) * len(shape))


class Line:
    def __init__(self, here):
        self.here = here
        self.token = None
        self.arrived = []

    def call(self, body, grid, ins, in_specs, out_shape, out_specs, aliases=None):
        ins, in_specs = list(ins), list(in_specs)
        count = len(ins)
        order = ([] if self.token is None else [self.token]) + self.arrived
        taken = len(order)
        ins += order
        in_specs += [whole(*(1,) * (array.ndim - 2), 8, 128) for array in order]

        def run(here, *refs):
            refs[-1][...] = jnp.zeros((8, 128), F32)
            body(here, *refs[:count], *refs[count + taken : -1])

        *outs, self.token = pl.pallas_call(
            run,
            grid_spec=pltpu.PrefetchScalarGridSpec(
                num_scalar_prefetch=1,
                grid=(grid,),
                in_specs=in_specs,
                out_specs=(*out_specs, whole(8, 128)),
            ),
            out_shape=(*out_shape, jax.ShapeDtypeStruct((8, 128), F32)),
            input_output_aliases=aliases or {},
            compiler_params=pltpu.CompilerParams(vmem_limit_bytes=VMEM_LIMIT),
            cost_estimate=pl.CostEstimate(flops=0, bytes_accessed=0, transcendentals=0),
        )(self.here, *ins)
        return outs


def tiles(n, *groups):
    for tile in range(n):
        yield slice(tile * TILE, (tile + 1) * TILE), [group[tile] for group in groups]


def groups(refs, n):
    return [refs[k : k + n] for k in range(0, len(refs), n)]


def send_part(line, half, partials, up_from, down_from):
    w, n = half.width, half.count

    def body(here, *refs):
        up, down = refs[2 * n :]
        for col, (part_up, part_down) in tiles(n, *groups(refs[: 2 * n], n)):
            up[:, col] = part_up[...].astype(F32)
            down[:, col] = part_down[...].astype(F32)

    shape = jax.ShapeDtypeStruct((HALF, SIDE * w), F32)
    spec = pl.BlockSpec((HALF, w), lambda i, here: (0, i))
    return line.call(
        body, SIDE, [partials] * (2 * n), half.grid_blocks(*up_from) + half.grid_blocks(*down_from),
        (shape, shape), (spec, spec),
    )


def send_far(line, half, partials):
    return send_part(line, half, partials, (2, 0), (2, 1))


def send_raw(line, half, partials):
    return send_part(line, half, partials, (1, 1), (-1, 0))


def send_near(line, half, partials, far_up, far_down):
    w, n = half.width, half.count

    def body(here, *refs):
        far_up, far_down, up, down = refs[2 * n :]
        for col, (part_up, part_down) in tiles(n, *groups(refs[: 2 * n], n)):
            up[:, col] = part_up[...].astype(F32) + far_up[:, col]
            down[:, col] = part_down[...].astype(F32) + far_down[:, col]

    shape = jax.ShapeDtypeStruct((HALF, SIDE * w), F32)
    spec = pl.BlockSpec((HALF, w), lambda i, here: (0, i))
    return line.call(
        body, SIDE, [partials] * (2 * n) + [far_up, far_down],
        half.grid_blocks(1, 0) + half.grid_blocks(-1, 1) + [spec, spec],
        (shape, shape), (spec, spec),
    )


def repeat(arrays, n):
    return [array for array in arrays for _ in range(n)]


def high_low(part, raw_up, raw_down, near_up, near_down):
    high = part[:HALF].astype(F32) + near_up[...] + raw_down[...]
    low = part[HALF:].astype(F32) + near_down[...] + raw_up[...]
    return high, low


def send_far2(line, half, partials, got):
    w, n = half.width, half.count

    def body(here, *refs):
        up, down = refs[-2:]
        for col, blocks in tiles(n, *groups(refs[: 5 * n], n)):
            up[:, col], down[:, col] = high_low(*blocks)

    shape = jax.ShapeDtypeStruct((HALF, w), F32)
    return line.call(
        body, 1, [partials] * n + repeat(got, n), half.one_blocks(2) + half.message_blocks(2) * 4,
        (shape, shape), (whole(HALF, w), whole(HALF, w)),
    )


def send_near2(line, half, partials, got, far, first, n):
    own = slice(first, first + n)

    def body(here, *refs):
        up, down = refs[-2:]
        for col, blocks in tiles(n, *groups(refs[: 12 * n], n)):
            high, low = high_low(*blocks[:5])
            up[:HALF, col] = high + blocks[10][...]
            up[HALF:, col] = low
            high, low = high_low(*blocks[5:10])
            down[:HALF, col] = high
            down[HALF:, col] = low + blocks[11][...]

    far_specs = [pl.BlockSpec((HALF, TILE), lambda i, here, t=t: (0, t)) for t in range(half.count)]
    w = n * TILE
    shape = jax.ShapeDtypeStruct((BLOCK, w), F32)
    return line.call(
        body, 1, ([partials] * n + repeat(got, n)) * 2 + repeat(far, n),
        half.one_blocks(1)[own] + half.message_blocks(1)[own] * 4 + half.one_blocks(-1)[own]
        + half.message_blocks(-1)[own] * 4 + far_specs[own] * 2,
        (shape, shape), (whole(BLOCK, w), whole(BLOCK, w)),
    )


def product(parts, value):
    high = value.astype(BF16)
    low = (value - high.astype(F32)).astype(BF16)
    return jnp.dot(
        parts[...], jnp.concatenate([high, low, high, low], axis=0), preferred_element_type=F32
    )


def settle(grad_of, momentum, positions, forward, backward, fresh, values):
    for at in range(0, fresh.shape[2], CHUNK):
        col = slice(at, at + CHUNK)
        moment = 0.9 * momentum[0, :, col] + grad_of(col)
        coeff = product(forward, moment)
        chosen = positions[0, :, col]
        freq = lax.broadcasted_iota(jnp.int32, coeff.shape, 0)
        own = jnp.zeros_like(coeff)
        rows = []
        for place in range(KEEP):
            hit = jnp.where(chosen[place : place + 1] == freq, coeff, 0.0)
            rows.append(jnp.sum(hit, axis=0, keepdims=True))
            own = own + hit
        values[:, col] = jnp.concatenate(rows, axis=0)
        fresh[0, :, col] = moment - product(backward, own)


class Part:
    def __init__(self, pair, first, width, tile):
        self.pair, self.tile = pair, tile
        self.first, self.n, self.count = first // tile, width // tile, pair[0].width // tile
        self.steps, self.spans = 2 * self.n, 2 * width

    def place(self, i):
        return jnp.where(i < self.n, i, i - self.n + self.count) + self.first

    def columns(self, rows):
        return pl.BlockSpec((1, rows, self.tile), lambda i, here: (0, 0, self.place(i)))

    def result(self):
        return pl.BlockSpec((BLOCK, self.tile), lambda i, here: (0, self.place(i)))

    def compact(self, rows):
        return pl.BlockSpec((rows, self.tile), lambda i, here: (0, i))


def finish(line, piece, partials, momentum, positions, got, tables, so_far):
    n = piece.n
    ins, specs = [], []
    for number, (half, arrays) in enumerate(zip(piece.pair, got)):
        ins += [partials, *arrays]

        def tile(i, number=number):
            return jnp.minimum(i, n - 1) if number == 0 else jnp.maximum(i - n, 0)

        def part(i, here, half=half, tile=tile):
            target = half.column(here, 0, half.second(here, 0)) * (TILE // piece.tile)
            return 0, target + piece.first + tile(i)

        def message(i, here, half=half, tile=tile):
            return 0, half.second(here, 0) * piece.count + piece.first + tile(i)

        def flat(i, here, tile=tile):
            return 0, tile(i)

        specs += [pl.BlockSpec((BLOCK, piece.tile), part)]
        specs += [pl.BlockSpec((HALF, piece.tile), message)] * 4
        specs += [pl.BlockSpec((BLOCK, piece.tile), flat)] * 2
    ins += [momentum, positions, *tables]
    specs += [piece.columns(BLOCK), piece.columns(KEEP)] + [whole(BLOCK, 4 * BLOCK)] * 2
    aliases = {}
    if so_far is not None:
        ins.append(so_far)
        specs.append(pl.BlockSpec(memory_space=pl.ANY))
        aliases = {len(ins): 0}

    def body(here, *refs):
        momentum, positions, forward, backward = refs[14:18]

        def half(part, raw_up, raw_down, near_up, near_down, left2, right2):
            def grad_of(col):
                first = (raw_up, raw_down, near_up, near_down)
                pair = high_low(part[:, col], *(ref[:, col] for ref in first))
                return jnp.concatenate(pair, axis=0) + left2[:, col] + right2[:, col]

            settle(grad_of, momentum, positions, forward, backward, *refs[-2:])

        @pl.when(pl.program_id(0) < n)
        def _():
            half(*refs[0:7])

        @pl.when(pl.program_id(0) >= n)
        def _():
            half(*refs[7:14])

    return line.call(
        body, piece.steps, ins, specs,
        (jax.ShapeDtypeStruct(momentum.shape, F32), jax.ShapeDtypeStruct((KEEP, piece.spans), F32)),
        (piece.columns(BLOCK), piece.compact(KEEP)), aliases=aliases,
    )


def dense(values, chosen):
    freq = lax.broadcasted_iota(jnp.int32, (BLOCK, values.shape[1]), 0)
    acc = jnp.zeros((BLOCK, values.shape[1]), F32)
    for place in range(KEEP):
        acc = jnp.where(chosen[place : place + 1] == freq, values[place : place + 1], acc)
    return acc


def spread(line, piece, lists, places, table):
    def body(here, *refs):
        backward, out = refs[-2:]
        for at in range(0, piece.tile, CHUNK):
            col = slice(at, at + CHUNK)
            parts = [dense(refs[k][:, col], refs[4 + k][0, :, col]) for k in range(4)]
            out[:, col] = product(backward, (parts[0] + parts[1 + STEPS.index(2)]) + (parts[1 + STEPS.index(1)] + parts[1 + STEPS.index(-1)]))

    return line.call(
        body, piece.steps, [*lists, *places, table],
        [piece.compact(KEEP)] * 4 + [piece.columns(KEEP)] * 4 + [whole(BLOCK, 4 * BLOCK)],
        (jax.ShapeDtypeStruct((BLOCK, piece.spans), F32),), (piece.compact(BLOCK),),
    )[0]


def join(line, piece, mine, other, spans, so_far):
    ins, specs, aliases = [mine, other], [piece.compact(BLOCK)] * 2, {}
    if so_far is not None:
        ins.append(so_far)
        specs.append(pl.BlockSpec(memory_space=pl.ANY))
        aliases = {3: 0}

    def body(here, *refs):
        refs[-1][...] = refs[0][...] + refs[1][...]

    return line.call(
        body, piece.steps, ins, specs, (jax.ShapeDtypeStruct((BLOCK, spans), F32),),
        (piece.result(),), aliases=aliases,
    )[0]


def shift(dy, dx):
    return [
        (y * SIDE + x, (y + dy) % SIDE * SIDE + (x + dx) % SIDE)
        for y in range(SIDE)
        for x in range(SIDE)
    ]


def along(x_first, value, step):
    return lax.ppermute(value, "fsdp", shift(0, step) if x_first else shift(step, 0))


def along_z(value, step):
    return lax.ppermute(
        value, "rep", [(z * 2 + c, (z + step) % SIDE * 2 + c) for z in range(SIDE) for c in range(2)]
    )


def other_core(value):
    return lax.ppermute(value, "rep", [(r, r ^ 1) for r in range(2 * SIDE)])


def both(x_first, sent):
    return [along(x_first, sent[0], 1), along(x_first, sent[1], -1)]


def on_device(partials, momentum, positions):
    spans = momentum.shape[2]
    flat = partials.reshape(partials.shape[2:])
    me = lax.axis_index("fsdp")
    here = jnp.stack([me // SIDE, lax.rem(me, SIDE)]).astype(jnp.int32)
    tables = tuple(jnp.asarray(part) for part in dct_parts())
    line = Line(here)
    places = [positions] + [along_z(positions, step) for step in STEPS]
    width = spans // 2
    pair = (Half(True, 0, width, spans), Half(False, width, width, spans))
    ends = [TILE * sum(PARTS[:number]) for number in range(len(PARTS) + 1)]
    spaces = list(zip(ends, ends[1:]))
    got, sent = {}, []

    def each(stage, second, send):
        number = len(sent)
        out = [None, None]
        for axis in (AXES[number], 1 - AXES[number]):
            h = 1 - axis if second else axis
            line.arrived = sent[number - LAG[number]][axis] if number >= LAG[number] else []
            out[h] = both(axis == 0, send(pair[h], h))
        line.arrived = []
        got[stage] = out
        messages = out[::-1] if second else out
        sent.append([
            messages[axis] + [p for p, w in zip(places[1:], PLACES_WITH) if w == (number, axis)]
            for axis in range(2)
        ])

    def before(h, *stages):
        return sum((got[stage][h] for stage in stages), [])

    each("far", False, lambda half, h: send_far(line, half, flat))
    each("raw", False, lambda half, h: send_raw(line, half, flat))
    each("near", False, lambda half, h: send_near(line, half, flat, *before(h, "far")))
    each("far2", True, lambda half, h: send_far2(line, half, flat, before(h, "raw", "near")))
    for number, (first, end) in enumerate(spaces):
        each(
            number, True,
            lambda half, h: send_near2(
                line, half, flat, before(h, "raw", "near"), before(h, "far2"), first // TILE, (end - first) // TILE
            ),
        )
    fresh = update = None
    lists, mine = {}, {}
    for what, number in TAIL:
        number = int(number)
        first, end = spaces[number]
        piece = Part(pair, first, end - first, dict(f=FINE, s=TILE, j=BROAD)[what])
        if what == "f":
            full = [before(h, "raw", "near", number) for h in range(2)]
            fresh, own = finish(line, piece, flat, momentum, positions, full, tables, fresh)
            lists[number] = [own] + [along_z(own, step) for step in STEPS]
        elif what == "s":
            part = spread(line, piece, lists[number], places, tables[1])
            mine[number] = part, other_core(part)
        else:
            update = join(line, piece, *mine[number], spans, update)
    return update, fresh


def solution(mesh):
    placed = (P("rep", "fsdp", None, None), P("rep", None, "fsdp"), P("rep", None, "fsdp"))
    return jax.shard_map(
        on_device,
        mesh=mesh,
        in_specs=placed,
        out_specs=(P(None, "fsdp"), P("rep", None, "fsdp")),
        check_vma=False,
    )
```

```python
import jax
import jax.numpy as jnp
import ml_dtypes
import numpy as np
from jax import lax
from jax.experimental import pallas as pl
from jax.experimental.pallas import tpu as pltpu
from jax.sharding import PartitionSpec as P

BLOCK = 64
HALF = BLOCK // 2
KEEP = 8
SIDE = 4
TILE = 1024
CHUNK = 256
FINE, BROAD = 1024, 1024
PARTS = (2, 2)
AXES = (0, 0, 0, 1, 1, 0)
LAG = (2, 2, 2, 2, 2, 2)
PLACES_WITH = ((0, 1), (1, 0), (1, 0))
STEPS = (1, -1, 2)
TAIL = ("f0", "f1", "s0", "s1", "j0", "j1")
VMEM_LIMIT = 48 * 1024 * 1024
F32 = jnp.float32
BF16 = jnp.bfloat16


def dct_parts():
    k = np.arange(BLOCK, dtype=np.float64)[:, None]
    n = np.arange(BLOCK, dtype=np.float64)[None, :]
    scale = np.where(k == 0, np.sqrt(1.0 / BLOCK), np.sqrt(2.0 / BLOCK))
    dct = scale * np.cos(np.pi * (2.0 * n + 1.0) * k / (2.0 * BLOCK))

    def wide(mat):
        high = mat.astype(ml_dtypes.bfloat16)
        low = (mat - high.astype(np.float64)).astype(ml_dtypes.bfloat16)
        return np.concatenate([high, high, low, low], axis=1)

    return wide(dct), wide(dct.T.copy())


def fold(coord, step):
    return lax.rem(coord + (step + SIDE), SIDE)


class Half:
    def __init__(self, x_first, start, width, spans):
        self.x_first = x_first
        self.width = width
        self.count = width // TILE
        self.first = start // TILE
        self.per_target = spans // TILE

    def column(self, here, step, other):
        y, x = here[0], here[1]
        if self.x_first:
            target = other * SIDE + fold(x, step)
        else:
            target = fold(y, step) * SIDE + other
        return target * self.per_target + self.first

    def second(self, here, step):
        return fold(here[0] if self.x_first else here[1], step)

    def grid_blocks(self, step, rows):
        def spec(tile):
            return pl.BlockSpec(
                (HALF, TILE), lambda i, here: (rows, self.column(here, step, i) + tile)
            )

        return [spec(tile) for tile in range(self.count)]

    def one_blocks(self, step):
        def spec(tile):
            return pl.BlockSpec(
                (BLOCK, TILE),
                lambda i, here: (0, self.column(here, 0, self.second(here, step)) + tile),
            )

        return [spec(tile) for tile in range(self.count)]

    def message_blocks(self, step):
        def spec(tile):
            return pl.BlockSpec(
                (HALF, TILE), lambda i, here: (0, self.second(here, step) * self.count + tile)
            )

        return [spec(tile) for tile in range(self.count)]


def whole(*shape):
    return pl.BlockSpec(shape, lambda i, here: (0,) * len(shape))


class Line:
    def __init__(self, here):
        self.here = here
        self.token = None
        self.arrived = []

    def call(self, body, grid, ins, in_specs, out_shape, out_specs, aliases=None):
        ins, in_specs = list(ins), list(in_specs)
        count = len(ins)
        order = ([] if self.token is None else [self.token]) + self.arrived
        taken = len(order)
        ins += order
        in_specs += [whole(*(1,) * (array.ndim - 2), 8, 128) for array in order]

        def run(here, *refs):
            refs[-1][...] = jnp.zeros((8, 128), F32)
            body(here, *refs[:count], *refs[count + taken : -1])

        *outs, self.token = pl.pallas_call(
            run,
            grid_spec=pltpu.PrefetchScalarGridSpec(
                num_scalar_prefetch=1,
                grid=(grid,),
                in_specs=in_specs,
                out_specs=(*out_specs, whole(8, 128)),
            ),
            out_shape=(*out_shape, jax.ShapeDtypeStruct((8, 128), F32)),
            input_output_aliases=aliases or {},
            compiler_params=pltpu.CompilerParams(vmem_limit_bytes=VMEM_LIMIT),
            cost_estimate=pl.CostEstimate(flops=0, bytes_accessed=0, transcendentals=0),
        )(self.here, *ins)
        return outs


def tiles(n, *groups):
    for tile in range(n):
        yield slice(tile * TILE, (tile + 1) * TILE), [group[tile] for group in groups]


def groups(refs, n):
    return [refs[k : k + n] for k in range(0, len(refs), n)]


def send_part(line, half, partials, up_from, down_from):
    w, n = half.width, half.count

    def body(here, *refs):
        up, down = refs[2 * n :]
        for col, (part_up, part_down) in tiles(n, *groups(refs[: 2 * n], n)):
            up[:, col] = part_up[...].astype(F32)
            down[:, col] = part_down[...].astype(F32)

    shape = jax.ShapeDtypeStruct((HALF, SIDE * w), F32)
    spec = pl.BlockSpec((HALF, w), lambda i, here: (0, i))
    return line.call(
        body, SIDE, [partials] * (2 * n), half.grid_blocks(*up_from) + half.grid_blocks(*down_from),
        (shape, shape), (spec, spec),
    )


def send_far(line, half, partials):
    return send_part(line, half, partials, (2, 0), (2, 1))


def send_raw(line, half, partials):
    return send_part(line, half, partials, (1, 1), (-1, 0))


def send_near(line, half, partials, far_up, far_down):
    w, n = half.width, half.count

    def body(here, *refs):
        far_up, far_down, up, down = refs[2 * n :]
        for col, (part_up, part_down) in tiles(n, *groups(refs[: 2 * n], n)):
            up[:, col] = part_up[...].astype(F32) + far_up[:, col]
            down[:, col] = part_down[...].astype(F32) + far_down[:, col]

    shape = jax.ShapeDtypeStruct((HALF, SIDE * w), F32)
    spec = pl.BlockSpec((HALF, w), lambda i, here: (0, i))
    return line.call(
        body, SIDE, [partials] * (2 * n) + [far_up, far_down],
        half.grid_blocks(1, 0) + half.grid_blocks(-1, 1) + [spec, spec],
        (shape, shape), (spec, spec),
    )


def repeat(arrays, n):
    return [array for array in arrays for _ in range(n)]


def high_low(part, raw_up, raw_down, near_up, near_down):
    high = part[:HALF].astype(F32) + near_up[...] + raw_down[...]
    low = part[HALF:].astype(F32) + near_down[...] + raw_up[...]
    return high, low


def send_far2(line, half, partials, got):
    w, n = half.width, half.count

    def body(here, *refs):
        up, down = refs[-2:]
        for col, blocks in tiles(n, *groups(refs[: 5 * n], n)):
            up[:, col], down[:, col] = high_low(*blocks)

    shape = jax.ShapeDtypeStruct((HALF, w), F32)
    return line.call(
        body, 1, [partials] * n + repeat(got, n), half.one_blocks(2) + half.message_blocks(2) * 4,
        (shape, shape), (whole(HALF, w), whole(HALF, w)),
    )


def send_near2(line, half, partials, got, far, first, n):
    own = slice(first, first + n)

    def body(here, *refs):
        up, down = refs[-2:]
        for col, blocks in tiles(n, *groups(refs[: 12 * n], n)):
            high, low = high_low(*blocks[:5])
            up[:HALF, col] = high + blocks[10][...]
            up[HALF:, col] = low
            high, low = high_low(*blocks[5:10])
            down[:HALF, col] = high
            down[HALF:, col] = low + blocks[11][...]

    far_specs = [pl.BlockSpec((HALF, TILE), lambda i, here, t=t: (0, t)) for t in range(half.count)]
    w = n * TILE
    shape = jax.ShapeDtypeStruct((BLOCK, w), F32)
    return line.call(
        body, 1, ([partials] * n + repeat(got, n)) * 2 + repeat(far, n),
        half.one_blocks(1)[own] + half.message_blocks(1)[own] * 4 + half.one_blocks(-1)[own]
        + half.message_blocks(-1)[own] * 4 + far_specs[own] * 2,
        (shape, shape), (whole(BLOCK, w), whole(BLOCK, w)),
    )


def product(parts, value):
    high = value.astype(BF16)
    low = (value - high.astype(F32)).astype(BF16)
    return jnp.dot(
        parts[...], jnp.concatenate([high, low, high, low], axis=0), preferred_element_type=F32
    )


def settle(grad_of, momentum, positions, forward, backward, fresh, values):
    for at in range(0, fresh.shape[2], CHUNK):
        col = slice(at, at + CHUNK)
        moment = 0.9 * momentum[0, :, col] + grad_of(col)
        coeff = product(forward, moment)
        chosen = positions[0, :, col]
        freq = lax.broadcasted_iota(jnp.int32, coeff.shape, 0)
        own = jnp.zeros_like(coeff)
        rows = []
        for place in range(KEEP):
            hit = jnp.where(chosen[place : place + 1] == freq, coeff, 0.0)
            rows.append(jnp.sum(hit, axis=0, keepdims=True))
            own = own + hit
        values[:, col] = jnp.concatenate(rows, axis=0)
        fresh[0, :, col] = moment - product(backward, own)


class Part:
    def __init__(self, pair, first, width, tile):
        self.pair, self.tile = pair, tile
        self.first, self.n, self.count = first // tile, width // tile, pair[0].width // tile
        self.steps, self.spans = 2 * self.n, 2 * width

    def place(self, i):
        return jnp.where(i < self.n, i, i - self.n + self.count) + self.first

    def columns(self, rows):
        return pl.BlockSpec((1, rows, self.tile), lambda i, here: (0, 0, self.place(i)))

    def result(self):
        return pl.BlockSpec((BLOCK, self.tile), lambda i, here: (0, self.place(i)))

    def compact(self, rows):
        return pl.BlockSpec((rows, self.tile), lambda i, here: (0, i))


def finish(line, piece, partials, momentum, positions, got, tables, so_far):
    n = piece.n
    ins, specs = [], []
    for number, (half, arrays) in enumerate(zip(piece.pair, got)):
        ins += [partials, *arrays]

        def tile(i, number=number):
            return jnp.minimum(i, n - 1) if number == 0 else jnp.maximum(i - n, 0)

        def part(i, here, half=half, tile=tile):
            target = half.column(here, 0, half.second(here, 0)) * (TILE // piece.tile)
            return 0, target + piece.first + tile(i)

        def message(i, here, half=half, tile=tile):
            return 0, half.second(here, 0) * piece.count + piece.first + tile(i)

        def flat(i, here, tile=tile):
            return 0, tile(i)

        specs += [pl.BlockSpec((BLOCK, piece.tile), part)]
        specs += [pl.BlockSpec((HALF, piece.tile), message)] * 4
        specs += [pl.BlockSpec((BLOCK, piece.tile), flat)] * 2
    ins += [momentum, positions, *tables]
    specs += [piece.columns(BLOCK), piece.columns(KEEP)] + [whole(BLOCK, 4 * BLOCK)] * 2
    aliases = {}
    if so_far is not None:
        ins.append(so_far)
        specs.append(pl.BlockSpec(memory_space=pl.ANY))
        aliases = {len(ins): 0}

    def body(here, *refs):
        momentum, positions, forward, backward = refs[14:18]

        def half(part, raw_up, raw_down, near_up, near_down, left2, right2):
            def grad_of(col):
                first = (raw_up, raw_down, near_up, near_down)
                pair = high_low(part[:, col], *(ref[:, col] for ref in first))
                return jnp.concatenate(pair, axis=0) + left2[:, col] + right2[:, col]

            settle(grad_of, momentum, positions, forward, backward, *refs[-2:])

        @pl.when(pl.program_id(0) < n)
        def _():
            half(*refs[0:7])

        @pl.when(pl.program_id(0) >= n)
        def _():
            half(*refs[7:14])

    return line.call(
        body, piece.steps, ins, specs,
        (jax.ShapeDtypeStruct(momentum.shape, F32), jax.ShapeDtypeStruct((KEEP, piece.spans), F32)),
        (piece.columns(BLOCK), piece.compact(KEEP)), aliases=aliases,
    )


def dense(values, chosen):
    freq = lax.broadcasted_iota(jnp.int32, (BLOCK, values.shape[1]), 0)
    acc = jnp.zeros((BLOCK, values.shape[1]), F32)
    for place in range(KEEP):
        acc = jnp.where(chosen[place : place + 1] == freq, values[place : place + 1], acc)
    return acc


def spread(line, piece, lists, places, table):
    def body(here, *refs):
        backward, out = refs[-2:]
        for at in range(0, piece.tile, CHUNK):
            col = slice(at, at + CHUNK)
            parts = [dense(refs[k][:, col], refs[4 + k][0, :, col]) for k in range(4)]
            out[:, col] = product(backward, (parts[0] + parts[1 + STEPS.index(2)]) + (parts[1 + STEPS.index(1)] + parts[1 + STEPS.index(-1)]))

    return line.call(
        body, piece.steps, [*lists, *places, table],
        [piece.compact(KEEP)] * 4 + [piece.columns(KEEP)] * 4 + [whole(BLOCK, 4 * BLOCK)],
        (jax.ShapeDtypeStruct((BLOCK, piece.spans), F32),), (piece.compact(BLOCK),),
    )[0]


def join(line, piece, mine, other, spans, so_far):
    ins, specs, aliases = [mine, other], [piece.compact(BLOCK)] * 2, {}
    if so_far is not None:
        ins.append(so_far)
        specs.append(pl.BlockSpec(memory_space=pl.ANY))
        aliases = {3: 0}

    def body(here, *refs):
        refs[-1][...] = refs[0][...] + refs[1][...]

    return line.call(
        body, piece.steps, ins, specs, (jax.ShapeDtypeStruct((BLOCK, spans), F32),),
        (piece.result(),), aliases=aliases,
    )[0]


def shift(dy, dx):
    return [
        (y * SIDE + x, (y + dy) % SIDE * SIDE + (x + dx) % SIDE)
        for y in range(SIDE)
        for x in range(SIDE)
    ]


def along(x_first, value, step):
    return lax.ppermute(value, "fsdp", shift(0, step) if x_first else shift(step, 0))


def along_z(value, step):
    return lax.ppermute(
        value, "rep", [(z * 2 + c, (z + step) % SIDE * 2 + c) for z in range(SIDE) for c in range(2)]
    )


def other_core(value):
    return lax.ppermute(value, "rep", [(r, r ^ 1) for r in range(2 * SIDE)])


def both(x_first, sent):
    return [along(x_first, sent[0], 1), along(x_first, sent[1], -1)]


def on_device(partials, momentum, positions):
    spans = momentum.shape[2]
    flat = partials.reshape(partials.shape[2:])
    me = lax.axis_index("fsdp")
    here = jnp.stack([me // SIDE, lax.rem(me, SIDE)]).astype(jnp.int32)
    tables = tuple(jnp.asarray(part) for part in dct_parts())
    line = Line(here)
    places = [positions] + [along_z(positions, step) for step in STEPS]
    width = spans // 2
    pair = (Half(True, 0, width, spans), Half(False, width, width, spans))
    ends = [TILE * sum(PARTS[:number]) for number in range(len(PARTS) + 1)]
    spaces = list(zip(ends, ends[1:]))
    got, sent = {}, []

    def each(stage, second, send):
        number = len(sent)
        out = [None, None]
        for axis in (AXES[number], 1 - AXES[number]):
            h = 1 - axis if second else axis
            line.arrived = sent[number - LAG[number]][axis] if number >= LAG[number] else []
            out[h] = both(axis == 0, send(pair[h], h))
        line.arrived = []
        got[stage] = out
        messages = out[::-1] if second else out
        sent.append([
            messages[axis] + [p for p, w in zip(places[1:], PLACES_WITH) if w == (number, axis)]
            for axis in range(2)
        ])

    def before(h, *stages):
        return sum((got[stage][h] for stage in stages), [])

    each("far", False, lambda half, h: send_far(line, half, flat))
    each("raw", False, lambda half, h: send_raw(line, half, flat))
    each("near", False, lambda half, h: send_near(line, half, flat, *before(h, "far")))
    each("far2", True, lambda half, h: send_far2(line, half, flat, before(h, "raw", "near")))
    for number, (first, end) in enumerate(spaces):
        each(
            number, True,
            lambda half, h: send_near2(
                line, half, flat, before(h, "raw", "near"), before(h, "far2"), first // TILE, (end - first) // TILE
            ),
        )
    fresh = update = None
    lists, mine = {}, {}
    for what, number in TAIL:
        number = int(number)
        first, end = spaces[number]
        piece = Part(pair, first, end - first, dict(f=FINE, s=TILE, j=BROAD)[what])
        if what == "f":
            full = [before(h, "raw", "near", number) for h in range(2)]
            fresh, own = finish(line, piece, flat, momentum, positions, full, tables, fresh)
            lists[number] = [own] + [along_z(own, step) for step in STEPS]
        elif what == "s":
            part = spread(line, piece, lists[number], places, tables[1])
            mine[number] = part, other_core(part)
        else:
            update = join(line, piece, *mine[number], spans, update)
    return update, fresh


def solution(mesh):
    placed = (P("rep", "fsdp", None, None), P("rep", None, "fsdp"), P("rep", None, "fsdp"))
    return jax.shard_map(
        on_device,
        mesh=mesh,
        in_specs=placed,
        out_specs=(P(None, "fsdp"), P("rep", None, "fsdp")),
        check_vma=False,
    )
```

```python
import jax
import jax.numpy as jnp
import ml_dtypes
import numpy as np
from jax import lax
from jax.experimental import pallas as pl
from jax.experimental.pallas import tpu as pltpu
from jax.sharding import PartitionSpec as P

BLOCK = 64
HALF = BLOCK // 2
KEEP = 8
SIDE = 4
TILE = 1024
CHUNK = 256
FINE, BROAD = 1024, 2048
PARTS = (2, 2)
AXES = (0, 0, 0, 1, 1, 1)
LAG = (2, 2, 2, 2, 2, 2)
PLACES_WITH = ((0, 1), (1, 0), (1, 0))
STEPS = (1, -1, 2)
TAIL = ('f0', 'f1', 's0', 's1', 'j0', 'j1')
TOGETHER = 2
VMEM_LIMIT = 48 * 1024 * 1024
F32 = jnp.float32
BF16 = jnp.bfloat16


def dct_parts():
    k = np.arange(BLOCK, dtype=np.float64)[:, None]
    n = np.arange(BLOCK, dtype=np.float64)[None, :]
    scale = np.where(k == 0, np.sqrt(1.0 / BLOCK), np.sqrt(2.0 / BLOCK))
    dct = scale * np.cos(np.pi * (2.0 * n + 1.0) * k / (2.0 * BLOCK))

    def wide(mat):
        high = mat.astype(ml_dtypes.bfloat16)
        low = (mat - high.astype(np.float64)).astype(ml_dtypes.bfloat16)
        return np.concatenate([high, high, low, low], axis=1)

    return wide(dct), wide(dct.T.copy())


def fold(coord, step):
    return lax.rem(coord + (step + SIDE), SIDE)


class Half:
    def __init__(self, x_first, start, width, spans):
        self.x_first = x_first
        self.width = width
        self.count = width // TILE
        self.first = start // TILE
        self.per_target = spans // TILE

    def column(self, here, step, other):
        y, x = here[0], here[1]
        if self.x_first:
            target = other * SIDE + fold(x, step)
        else:
            target = fold(y, step) * SIDE + other
        return target * self.per_target + self.first

    def second(self, here, step):
        return fold(here[0] if self.x_first else here[1], step)

    def grid_blocks(self, step, rows):
        def spec(other, tile):
            return pl.BlockSpec(
                (HALF, TILE),
                lambda i, here: (rows, self.column(here, step, i * TOGETHER + other) + tile),
            )

        return [spec(other, tile) for other in range(TOGETHER) for tile in range(self.count)]

    def one_blocks(self, step):
        def spec(tile):
            return pl.BlockSpec(
                (BLOCK, TILE),
                lambda i, here: (0, self.column(here, 0, self.second(here, step)) + tile),
            )

        return [spec(tile) for tile in range(self.count)]

    def message_blocks(self, step):
        def spec(tile):
            return pl.BlockSpec(
                (HALF, TILE), lambda i, here: (0, self.second(here, step) * self.count + tile)
            )

        return [spec(tile) for tile in range(self.count)]


def whole(*shape):
    return pl.BlockSpec(shape, lambda i, here: (0,) * len(shape))


class Line:
    def __init__(self, here):
        self.here = here
        self.token = None
        self.arrived = []

    def call(self, body, grid, ins, in_specs, out_shape, out_specs, aliases=None):
        ins, in_specs = list(ins), list(in_specs)
        count = len(ins)
        order = ([] if self.token is None else [self.token]) + self.arrived
        taken = len(order)
        ins += order
        in_specs += [whole(*(1,) * (array.ndim - 2), 8, 128) for array in order]

        def run(here, *refs):
            refs[-1][...] = jnp.zeros((8, 128), F32)
            body(here, *refs[:count], *refs[count + taken : -1])

        *outs, self.token = pl.pallas_call(
            run,
            grid_spec=pltpu.PrefetchScalarGridSpec(
                num_scalar_prefetch=1,
                grid=(grid,),
                in_specs=in_specs,
                out_specs=(*out_specs, whole(8, 128)),
            ),
            out_shape=(*out_shape, jax.ShapeDtypeStruct((8, 128), F32)),
            input_output_aliases=aliases or {},
            compiler_params=pltpu.CompilerParams(vmem_limit_bytes=VMEM_LIMIT),
            cost_estimate=pl.CostEstimate(flops=0, bytes_accessed=0, transcendentals=0),
        )(self.here, *ins)
        return outs


def tiles(n, *groups):
    for tile in range(n):
        yield slice(tile * TILE, (tile + 1) * TILE), [group[tile] for group in groups]


def groups(refs, n):
    return [refs[k : k + n] for k in range(0, len(refs), n)]


def send_part(line, half, partials, up_from, down_from):
    n = half.count * TOGETHER

    def body(here, *refs):
        up, down = refs[2 * n :]
        for col, (part_up, part_down) in tiles(n, *groups(refs[: 2 * n], n)):
            up[:, col] = part_up[...].astype(F32)
            down[:, col] = part_down[...].astype(F32)

    shape = jax.ShapeDtypeStruct((HALF, SIDE * half.width), F32)
    spec = pl.BlockSpec((HALF, n * TILE), lambda i, here: (0, i))
    return line.call(
        body, SIDE // TOGETHER, [partials] * (2 * n),
        half.grid_blocks(*up_from) + half.grid_blocks(*down_from), (shape, shape), (spec, spec),
    )


def send_far(line, half, partials):
    return send_part(line, half, partials, (2, 0), (2, 1))


def send_raw(line, half, partials):
    return send_part(line, half, partials, (1, 1), (-1, 0))


def send_near(line, half, partials, far_up, far_down):
    n = half.count * TOGETHER

    def body(here, *refs):
        far_up, far_down, up, down = refs[2 * n :]
        for col, (part_up, part_down) in tiles(n, *groups(refs[: 2 * n], n)):
            up[:, col] = part_up[...].astype(F32) + far_up[:, col]
            down[:, col] = part_down[...].astype(F32) + far_down[:, col]

    shape = jax.ShapeDtypeStruct((HALF, SIDE * half.width), F32)
    spec = pl.BlockSpec((HALF, n * TILE), lambda i, here: (0, i))
    return line.call(
        body, SIDE // TOGETHER, [partials] * (2 * n) + [far_up, far_down],
        half.grid_blocks(1, 0) + half.grid_blocks(-1, 1) + [spec, spec],
        (shape, shape), (spec, spec),
    )


def repeat(arrays, n):
    return [array for array in arrays for _ in range(n)]


def high_low(part, raw_up, raw_down, near_up, near_down):
    high = part[:HALF].astype(F32) + near_up[...] + raw_down[...]
    low = part[HALF:].astype(F32) + near_down[...] + raw_up[...]
    return high, low


def send_far2(line, half, partials, got):
    w, n = half.width, half.count

    def body(here, *refs):
        up, down = refs[-2:]
        for col, blocks in tiles(n, *groups(refs[: 5 * n], n)):
            up[:, col], down[:, col] = high_low(*blocks)

    shape = jax.ShapeDtypeStruct((HALF, w), F32)
    return line.call(
        body, 1, [partials] * n + repeat(got, n), half.one_blocks(2) + half.message_blocks(2) * 4,
        (shape, shape), (whole(HALF, w), whole(HALF, w)),
    )


def send_near2(line, half, partials, got, far, first, n):
    own = slice(first, first + n)

    def body(here, *refs):
        up, down = refs[-2:]
        for col, blocks in tiles(n, *groups(refs[: 12 * n], n)):
            high, low = high_low(*blocks[:5])
            up[:HALF, col] = high + blocks[10][...]
            up[HALF:, col] = low
            high, low = high_low(*blocks[5:10])
            down[:HALF, col] = high
            down[HALF:, col] = low + blocks[11][...]

    far_specs = [pl.BlockSpec((HALF, TILE), lambda i, here, t=t: (0, t)) for t in range(half.count)]
    w = n * TILE
    shape = jax.ShapeDtypeStruct((BLOCK, w), F32)
    return line.call(
        body, 1, ([partials] * n + repeat(got, n)) * 2 + repeat(far, n),
        half.one_blocks(1)[own] + half.message_blocks(1)[own] * 4 + half.one_blocks(-1)[own]
        + half.message_blocks(-1)[own] * 4 + far_specs[own] * 2,
        (shape, shape), (whole(BLOCK, w), whole(BLOCK, w)),
    )


def product(parts, value):
    high = value.astype(BF16)
    low = (value - high.astype(F32)).astype(BF16)
    return jnp.dot(
        parts[...], jnp.concatenate([high, low, high, low], axis=0), preferred_element_type=F32
    )


def settle(grad_of, momentum, positions, forward, backward, fresh, values):
    for at in range(0, fresh.shape[2], CHUNK):
        col = slice(at, at + CHUNK)
        moment = 0.9 * momentum[0, :, col] + grad_of(col)
        coeff = product(forward, moment)
        chosen = positions[0, :, col]
        freq = lax.broadcasted_iota(jnp.int32, coeff.shape, 0)
        own = jnp.zeros_like(coeff)
        rows = []
        for place in range(KEEP):
            hit = jnp.where(chosen[place : place + 1] == freq, coeff, 0.0)
            rows.append(jnp.sum(hit, axis=0, keepdims=True))
            own = own + hit
        values[:, col] = jnp.concatenate(rows, axis=0)
        fresh[0, :, col] = moment - product(backward, own)


class Part:
    def __init__(self, pair, first, width, tile):
        self.pair, self.tile = pair, tile
        self.first, self.n, self.count = first // tile, width // tile, pair[0].width // tile
        self.steps, self.spans = 2 * self.n, 2 * width

    def place(self, i):
        return jnp.where(i < self.n, i, i - self.n + self.count) + self.first

    def columns(self, rows):
        return pl.BlockSpec((1, rows, self.tile), lambda i, here: (0, 0, self.place(i)))

    def result(self):
        return pl.BlockSpec((BLOCK, self.tile), lambda i, here: (0, self.place(i)))

    def compact(self, rows):
        return pl.BlockSpec((rows, self.tile), lambda i, here: (0, i))


def finish(line, piece, partials, momentum, positions, got, tables, so_far):
    n = piece.n
    ins, specs = [], []
    for number, (half, arrays) in enumerate(zip(piece.pair, got)):
        ins += [partials, *arrays]

        def tile(i, number=number):
            return jnp.minimum(i, n - 1) if number == 0 else jnp.maximum(i - n, 0)

        def part(i, here, half=half, tile=tile):
            target = half.column(here, 0, half.second(here, 0)) * (TILE // piece.tile)
            return 0, target + piece.first + tile(i)

        def message(i, here, half=half, tile=tile):
            return 0, half.second(here, 0) * piece.count + piece.first + tile(i)

        def flat(i, here, tile=tile):
            return 0, tile(i)

        specs += [pl.BlockSpec((BLOCK, piece.tile), part)]
        specs += [pl.BlockSpec((HALF, piece.tile), message)] * 4
        specs += [pl.BlockSpec((BLOCK, piece.tile), flat)] * 2
    ins += [momentum, positions, *tables]
    specs += [piece.columns(BLOCK), piece.columns(KEEP)] + [whole(BLOCK, 4 * BLOCK)] * 2
    aliases = {}
    if so_far is not None:
        ins.append(so_far)
        specs.append(pl.BlockSpec(memory_space=pl.ANY))
        aliases = {len(ins): 0}

    def body(here, *refs):
        momentum, positions, forward, backward = refs[14:18]

        def half(part, raw_up, raw_down, near_up, near_down, left2, right2):
            def grad_of(col):
                first = (raw_up, raw_down, near_up, near_down)
                pair = high_low(part[:, col], *(ref[:, col] for ref in first))
                return jnp.concatenate(pair, axis=0) + left2[:, col] + right2[:, col]

            settle(grad_of, momentum, positions, forward, backward, *refs[-2:])

        @pl.when(pl.program_id(0) < n)
        def _():
            half(*refs[0:7])

        @pl.when(pl.program_id(0) >= n)
        def _():
            half(*refs[7:14])

    return line.call(
        body, piece.steps, ins, specs,
        (jax.ShapeDtypeStruct(momentum.shape, F32), jax.ShapeDtypeStruct((KEEP, piece.spans), F32)),
        (piece.columns(BLOCK), piece.compact(KEEP)), aliases=aliases,
    )


def dense(values, chosen):
    freq = lax.broadcasted_iota(jnp.int32, (BLOCK, values.shape[1]), 0)
    acc = jnp.zeros((BLOCK, values.shape[1]), F32)
    for place in range(KEEP):
        acc = jnp.where(chosen[place : place + 1] == freq, values[place : place + 1], acc)
    return acc


def spread(line, piece, lists, places, table):
    def body(here, *refs):
        backward, out = refs[-2:]
        for at in range(0, piece.tile, CHUNK):
            col = slice(at, at + CHUNK)
            parts = [dense(refs[k][:, col], refs[4 + k][0, :, col]) for k in range(4)]
            out[:, col] = product(backward, (parts[0] + parts[1 + STEPS.index(2)]) + (parts[1 + STEPS.index(1)] + parts[1 + STEPS.index(-1)]))

    return line.call(
        body, piece.steps, [*lists, *places, table],
        [piece.compact(KEEP)] * 4 + [piece.columns(KEEP)] * 4 + [whole(BLOCK, 4 * BLOCK)],
        (jax.ShapeDtypeStruct((BLOCK, piece.spans), F32),), (piece.compact(BLOCK),),
    )[0]


def join(line, piece, mine, other, spans, so_far):
    ins, specs, aliases = [mine, other], [piece.compact(BLOCK)] * 2, {}
    if so_far is not None:
        ins.append(so_far)
        specs.append(pl.BlockSpec(memory_space=pl.ANY))
        aliases = {3: 0}

    def body(here, *refs):
        refs[-1][...] = refs[0][...] + refs[1][...]

    return line.call(
        body, piece.steps, ins, specs, (jax.ShapeDtypeStruct((BLOCK, spans), F32),),
        (piece.result(),), aliases=aliases,
    )[0]


def shift(dy, dx):
    return [
        (y * SIDE + x, (y + dy) % SIDE * SIDE + (x + dx) % SIDE)
        for y in range(SIDE)
        for x in range(SIDE)
    ]


def along(x_first, value, step):
    return lax.ppermute(value, "fsdp", shift(0, step) if x_first else shift(step, 0))


def along_z(value, step):
    return lax.ppermute(
        value, "rep", [(z * 2 + c, (z + step) % SIDE * 2 + c) for z in range(SIDE) for c in range(2)]
    )


def other_core(value):
    return lax.ppermute(value, "rep", [(r, r ^ 1) for r in range(2 * SIDE)])


def both(x_first, sent):
    return [along(x_first, sent[0], 1), along(x_first, sent[1], -1)]


def on_device(partials, momentum, positions):
    spans = momentum.shape[2]
    flat = partials.reshape(partials.shape[2:])
    me = lax.axis_index("fsdp")
    here = jnp.stack([me // SIDE, lax.rem(me, SIDE)]).astype(jnp.int32)
    tables = tuple(jnp.asarray(part) for part in dct_parts())
    line = Line(here)
    places = [positions] + [along_z(positions, step) for step in STEPS]
    width = spans // 2
    pair = (Half(True, 0, width, spans), Half(False, width, width, spans))
    ends = [TILE * sum(PARTS[:number]) for number in range(len(PARTS) + 1)]
    spaces = list(zip(ends, ends[1:]))
    got, sent = {}, []

    def each(stage, second, send):
        number = len(sent)
        out = [None, None]
        for axis in (AXES[number], 1 - AXES[number]):
            h = 1 - axis if second else axis
            line.arrived = sent[number - LAG[number]][axis] if number >= LAG[number] else []
            out[h] = both(axis == 0, send(pair[h], h))
        line.arrived = []
        got[stage] = out
        messages = out[::-1] if second else out
        sent.append([
            messages[axis] + [p for p, w in zip(places[1:], PLACES_WITH) if w == (number, axis)]
            for axis in range(2)
        ])

    def before(h, *stages):
        return sum((got[stage][h] for stage in stages), [])

    each("far", False, lambda half, h: send_far(line, half, flat))
    each("raw", False, lambda half, h: send_raw(line, half, flat))
    each("near", False, lambda half, h: send_near(line, half, flat, *before(h, "far")))
    each("far2", True, lambda half, h: send_far2(line, half, flat, before(h, "raw", "near")))
    for number, (first, end) in enumerate(spaces):
        each(
            number, True,
            lambda half, h: send_near2(
                line, half, flat, before(h, "raw", "near"), before(h, "far2"), first // TILE, (end - first) // TILE
            ),
        )
    fresh = update = None
    lists, mine = {}, {}
    for what, number in TAIL:
        number = int(number)
        first, end = spaces[number]
        piece = Part(pair, first, end - first, dict(f=FINE, s=TILE, j=BROAD)[what])
        if what == "f":
            full = [before(h, "raw", "near", number) for h in range(2)]
            fresh, own = finish(line, piece, flat, momentum, positions, full, tables, fresh)
            lists[number] = [own] + [along_z(own, step) for step in STEPS]
        elif what == "s":
            part = spread(line, piece, lists[number], places, tables[1])
            mine[number] = part, other_core(part)
        else:
            update = join(line, piece, *mine[number], spans, update)
    return update, fresh


def solution(mesh):
    placed = (P("rep", "fsdp", None, None), P("rep", None, "fsdp"), P("rep", None, "fsdp"))
    return jax.shard_map(
        on_device,
        mesh=mesh,
        in_specs=placed,
        out_specs=(P(None, "fsdp"), P("rep", None, "fsdp")),
        check_vma=False,
    )
```

```python
import jax
import jax.numpy as jnp
import ml_dtypes
import numpy as np
from jax import lax
from jax.experimental import pallas as pl
from jax.experimental.pallas import tpu as pltpu
from jax.sharding import PartitionSpec as P

BLOCK = 64
HALF = BLOCK // 2
KEEP = 8
SIDE = 4
TILE = 1024
CHUNK = 256
FINE, BROAD = 1024, 2048
PARTS = (2, 2)
AXES = (0, 0, 0, 1, 1, 0)
LAG = (2, 2, 2, 2, 2, 2)
PLACES_WITH = ((0, 1), (1, 0))
TAIL = ('f0', 'f1', 's0', 's1', 'j0', 'j1')
TOGETHER = 1
VMEM_LIMIT = 48 * 1024 * 1024
F32 = jnp.float32
BF16 = jnp.bfloat16


def dct_parts():
    k = np.arange(BLOCK, dtype=np.float64)[:, None]
    n = np.arange(BLOCK, dtype=np.float64)[None, :]
    scale = np.where(k == 0, np.sqrt(1.0 / BLOCK), np.sqrt(2.0 / BLOCK))
    dct = scale * np.cos(np.pi * (2.0 * n + 1.0) * k / (2.0 * BLOCK))

    def wide(mat):
        high = mat.astype(ml_dtypes.bfloat16)
        low = (mat - high.astype(np.float64)).astype(ml_dtypes.bfloat16)
        return np.concatenate([high, high, low, low], axis=1)

    return wide(dct), wide(dct.T.copy())


def fold(coord, step):
    return lax.rem(coord + (step + SIDE), SIDE)


class Half:
    def __init__(self, x_first, start, width, spans):
        self.x_first = x_first
        self.width = width
        self.count = width // TILE
        self.first = start // TILE
        self.per_target = spans // TILE

    def column(self, here, step, other):
        y, x = here[0], here[1]
        if self.x_first:
            target = other * SIDE + fold(x, step)
        else:
            target = fold(y, step) * SIDE + other
        return target * self.per_target + self.first

    def second(self, here, step):
        return fold(here[0] if self.x_first else here[1], step)

    def grid_blocks(self, step, rows):
        def spec(other, tile):
            return pl.BlockSpec(
                (HALF, TILE),
                lambda i, here: (rows, self.column(here, step, i * TOGETHER + other) + tile),
            )

        return [spec(other, tile) for other in range(TOGETHER) for tile in range(self.count)]

    def one_blocks(self, step):
        def spec(tile):
            return pl.BlockSpec(
                (BLOCK, TILE),
                lambda i, here: (0, self.column(here, 0, self.second(here, step)) + tile),
            )

        return [spec(tile) for tile in range(self.count)]

    def message_blocks(self, step):
        def spec(tile):
            return pl.BlockSpec(
                (HALF, TILE), lambda i, here: (0, self.second(here, step) * self.count + tile)
            )

        return [spec(tile) for tile in range(self.count)]


def whole(*shape):
    return pl.BlockSpec(shape, lambda i, here: (0,) * len(shape))


class Line:
    def __init__(self, here):
        self.here = here
        self.token = None
        self.arrived = []

    def call(self, body, grid, ins, in_specs, out_shape, out_specs, aliases=None):
        ins, in_specs = list(ins), list(in_specs)
        count = len(ins)
        order = ([] if self.token is None else [self.token]) + self.arrived
        taken = len(order)
        ins += order
        in_specs += [whole(*(1,) * (array.ndim - 2), 8, 128) for array in order]

        def run(here, *refs):
            refs[-1][...] = jnp.zeros((8, 128), F32)
            body(here, *refs[:count], *refs[count + taken : -1])

        *outs, self.token = pl.pallas_call(
            run,
            grid_spec=pltpu.PrefetchScalarGridSpec(
                num_scalar_prefetch=1,
                grid=(grid,),
                in_specs=in_specs,
                out_specs=(*out_specs, whole(8, 128)),
            ),
            out_shape=(*out_shape, jax.ShapeDtypeStruct((8, 128), F32)),
            input_output_aliases=aliases or {},
            compiler_params=pltpu.CompilerParams(vmem_limit_bytes=VMEM_LIMIT),
            cost_estimate=pl.CostEstimate(flops=0, bytes_accessed=0, transcendentals=0),
        )(self.here, *ins)
        return outs


def tiles(n, *groups):
    for tile in range(n):
        yield slice(tile * TILE, (tile + 1) * TILE), [group[tile] for group in groups]


def groups(refs, n):
    return [refs[k : k + n] for k in range(0, len(refs), n)]


def send_part(line, half, partials, up_from, down_from):
    n = half.count * TOGETHER

    def body(here, *refs):
        up, down = refs[2 * n :]
        for col, (part_up, part_down) in tiles(n, *groups(refs[: 2 * n], n)):
            up[:, col] = part_up[...].astype(F32)
            down[:, col] = part_down[...].astype(F32)

    shape = jax.ShapeDtypeStruct((HALF, SIDE * half.width), F32)
    spec = pl.BlockSpec((HALF, n * TILE), lambda i, here: (0, i))
    return line.call(
        body, SIDE // TOGETHER, [partials] * (2 * n),
        half.grid_blocks(*up_from) + half.grid_blocks(*down_from), (shape, shape), (spec, spec),
    )


def send_far(line, half, partials):
    return send_part(line, half, partials, (2, 0), (2, 1))


def send_raw(line, half, partials):
    return send_part(line, half, partials, (1, 1), (-1, 0))


def send_near(line, half, partials, far_up, far_down):
    n = half.count * TOGETHER

    def body(here, *refs):
        far_up, far_down, up, down = refs[2 * n :]
        for col, (part_up, part_down) in tiles(n, *groups(refs[: 2 * n], n)):
            up[:, col] = part_up[...].astype(F32) + far_up[:, col]
            down[:, col] = part_down[...].astype(F32) + far_down[:, col]

    shape = jax.ShapeDtypeStruct((HALF, SIDE * half.width), F32)
    spec = pl.BlockSpec((HALF, n * TILE), lambda i, here: (0, i))
    return line.call(
        body, SIDE // TOGETHER, [partials] * (2 * n) + [far_up, far_down],
        half.grid_blocks(1, 0) + half.grid_blocks(-1, 1) + [spec, spec],
        (shape, shape), (spec, spec),
    )


def repeat(arrays, n):
    return [array for array in arrays for _ in range(n)]


def high_low(part, raw_up, raw_down, near_up, near_down):
    high = part[:HALF].astype(F32) + near_up[...] + raw_down[...]
    low = part[HALF:].astype(F32) + near_down[...] + raw_up[...]
    return high, low


def send_far2(line, half, partials, got):
    w, n = half.width, half.count

    def body(here, *refs):
        up, down = refs[-2:]
        for col, blocks in tiles(n, *groups(refs[: 5 * n], n)):
            up[:, col], down[:, col] = high_low(*blocks)

    shape = jax.ShapeDtypeStruct((HALF, w), F32)
    return line.call(
        body, 1, [partials] * n + repeat(got, n), half.one_blocks(2) + half.message_blocks(2) * 4,
        (shape, shape), (whole(HALF, w), whole(HALF, w)),
    )


def send_near2(line, half, partials, got, far, first, n):
    own = slice(first, first + n)

    def body(here, *refs):
        up, down = refs[-2:]
        for col, blocks in tiles(n, *groups(refs[: 12 * n], n)):
            high, low = high_low(*blocks[:5])
            up[:HALF, col] = high + blocks[10][...]
            up[HALF:, col] = low
            high, low = high_low(*blocks[5:10])
            down[:HALF, col] = high
            down[HALF:, col] = low + blocks[11][...]

    far_specs = [pl.BlockSpec((HALF, TILE), lambda i, here, t=t: (0, t)) for t in range(half.count)]
    w = n * TILE
    shape = jax.ShapeDtypeStruct((BLOCK, w), F32)
    return line.call(
        body, 1, ([partials] * n + repeat(got, n)) * 2 + repeat(far, n),
        half.one_blocks(1)[own] + half.message_blocks(1)[own] * 4 + half.one_blocks(-1)[own]
        + half.message_blocks(-1)[own] * 4 + far_specs[own] * 2,
        (shape, shape), (whole(BLOCK, w), whole(BLOCK, w)),
    )


def product(parts, value):
    high = value.astype(BF16)
    low = (value - high.astype(F32)).astype(BF16)
    return jnp.dot(
        parts[...], jnp.concatenate([high, low, high, low], axis=0), preferred_element_type=F32
    )


def settle(grad_of, momentum, positions, forward, backward, fresh, values):
    for at in range(0, fresh.shape[2], CHUNK):
        col = slice(at, at + CHUNK)
        moment = 0.9 * momentum[0, :, col] + grad_of(col)
        coeff = product(forward, moment)
        chosen = positions[0, :, col]
        freq = lax.broadcasted_iota(jnp.int32, coeff.shape, 0)
        own = jnp.zeros_like(coeff)
        rows = []
        for place in range(KEEP):
            hit = jnp.where(chosen[place : place + 1] == freq, coeff, 0.0)
            rows.append(jnp.sum(hit, axis=0, keepdims=True))
            own = own + hit
        values[:, col] = jnp.concatenate(rows, axis=0)
        fresh[0, :, col] = moment - product(backward, own)


class Part:
    def __init__(self, pair, first, width, tile):
        self.pair, self.tile = pair, tile
        self.first, self.n, self.count = first // tile, width // tile, pair[0].width // tile
        self.steps, self.spans = 2 * self.n, 2 * width

    def place(self, i):
        return jnp.where(i < self.n, i, i - self.n + self.count) + self.first

    def columns(self, rows, block=0):
        return pl.BlockSpec((1, rows, self.tile), lambda i, here: (0, block, self.place(i)))

    def result(self):
        return pl.BlockSpec((BLOCK, self.tile), lambda i, here: (0, self.place(i)))

    def compact(self, rows):
        return pl.BlockSpec((rows, self.tile), lambda i, here: (0, i))


def finish(line, piece, partials, momentum, positions, got, tables, so_far):
    n = piece.n
    ins, specs = [], []
    for number, (half, arrays) in enumerate(zip(piece.pair, got)):
        ins += [partials, *arrays]

        def tile(i, number=number):
            return jnp.minimum(i, n - 1) if number == 0 else jnp.maximum(i - n, 0)

        def part(i, here, half=half, tile=tile):
            target = half.column(here, 0, half.second(here, 0)) * (TILE // piece.tile)
            return 0, target + piece.first + tile(i)

        def message(i, here, half=half, tile=tile):
            return 0, half.second(here, 0) * piece.count + piece.first + tile(i)

        def flat(i, here, tile=tile):
            return 0, tile(i)

        specs += [pl.BlockSpec((BLOCK, piece.tile), part)]
        specs += [pl.BlockSpec((HALF, piece.tile), message)] * 4
        specs += [pl.BlockSpec((BLOCK, piece.tile), flat)] * 2
    ins += [momentum, positions, *tables]
    specs += [piece.columns(BLOCK), piece.columns(KEEP)] + [whole(BLOCK, 4 * BLOCK)] * 2
    aliases = {}
    if so_far is not None:
        ins.append(so_far)
        specs.append(pl.BlockSpec(memory_space=pl.ANY))
        aliases = {len(ins): 0}

    def body(here, *refs):
        momentum, positions, forward, backward = refs[14:18]

        def half(part, raw_up, raw_down, near_up, near_down, left2, right2):
            def grad_of(col):
                first = (raw_up, raw_down, near_up, near_down)
                pair = high_low(part[:, col], *(ref[:, col] for ref in first))
                return jnp.concatenate(pair, axis=0) + left2[:, col] + right2[:, col]

            settle(grad_of, momentum, positions, forward, backward, *refs[-2:])

        @pl.when(pl.program_id(0) < n)
        def _():
            half(*refs[0:7])

        @pl.when(pl.program_id(0) >= n)
        def _():
            half(*refs[7:14])

    return line.call(
        body, piece.steps, ins, specs,
        (jax.ShapeDtypeStruct(momentum.shape, F32), jax.ShapeDtypeStruct((KEEP, piece.spans), F32)),
        (piece.columns(BLOCK), piece.compact(KEEP)), aliases=aliases,
    )


def dense(values, chosen):
    freq = lax.broadcasted_iota(jnp.int32, (BLOCK, values.shape[1]), 0)
    acc = jnp.zeros((BLOCK, values.shape[1]), F32)
    for place in range(KEEP):
        acc = jnp.where(chosen[place : place + 1] == freq, values[place : place + 1], acc)
    return acc


def spread(line, piece, lists, places, table):
    def body(here, *refs):
        backward, out = refs[-2:]
        for at in range(0, piece.tile, CHUNK):
            col = slice(at, at + CHUNK)
            parts = [dense(refs[k][:, col], refs[4 + k][0, :, col]) for k in range(4)]
            out[:, col] = product(backward, (parts[0] + parts[3]) + (parts[1] + parts[2]))

    return line.call(
        body, piece.steps, [*lists, *(array for array, _ in places), table],
        [piece.compact(KEEP)] * 4 + [piece.columns(KEEP, block) for _, block in places]
        + [whole(BLOCK, 4 * BLOCK)],
        (jax.ShapeDtypeStruct((BLOCK, piece.spans), F32),), (piece.compact(BLOCK),),
    )[0]


def join(line, piece, mine, other, spans, so_far):
    ins, specs, aliases = [mine, other], [piece.compact(BLOCK)] * 2, {}
    if so_far is not None:
        ins.append(so_far)
        specs.append(pl.BlockSpec(memory_space=pl.ANY))
        aliases = {3: 0}

    def body(here, *refs):
        refs[-1][...] = refs[0][...] + refs[1][...]

    return line.call(
        body, piece.steps, ins, specs, (jax.ShapeDtypeStruct((BLOCK, spans), F32),),
        (piece.result(),), aliases=aliases,
    )[0]


def shift(dy, dx):
    return [
        (y * SIDE + x, (y + dy) % SIDE * SIDE + (x + dx) % SIDE)
        for y in range(SIDE)
        for x in range(SIDE)
    ]


def along(x_first, value, step):
    return lax.ppermute(value, "fsdp", shift(0, step) if x_first else shift(step, 0))


def along_z(value, step):
    return lax.ppermute(
        value, "rep", [(z * 2 + c, (z + step) % SIDE * 2 + c) for z in range(SIDE) for c in range(2)]
    )


def other_core(value):
    return lax.ppermute(value, "rep", [(r, r ^ 1) for r in range(2 * SIDE)])


def both(x_first, sent):
    return [along(x_first, sent[0], 1), along(x_first, sent[1], -1)]


def on_device(partials, momentum, positions):
    spans = momentum.shape[2]
    flat = partials.reshape(partials.shape[2:])
    me = lax.axis_index("fsdp")
    here = jnp.stack([me // SIDE, lax.rem(me, SIDE)]).astype(jnp.int32)
    tables = tuple(jnp.asarray(part) for part in dct_parts())
    line = Line(here)
    one_back = along_z(positions, 1)
    two_back = along_z(jnp.concatenate([positions, one_back], axis=1), 2)
    places = [(positions, 0), (one_back, 0), (two_back, 1), (two_back, 0)]
    width = spans // 2
    pair = (Half(True, 0, width, spans), Half(False, width, width, spans))
    ends = [TILE * sum(PARTS[:number]) for number in range(len(PARTS) + 1)]
    spaces = list(zip(ends, ends[1:]))
    got, sent = {}, []

    def each(stage, second, send):
        number = len(sent)
        out = [None, None]
        for axis in (AXES[number], 1 - AXES[number]):
            h = 1 - axis if second else axis
            line.arrived = sent[number - LAG[number]][axis] if number >= LAG[number] else []
            out[h] = both(axis == 0, send(pair[h], h))
        line.arrived = []
        got[stage] = out
        messages = out[::-1] if second else out
        sent.append([
            messages[axis] + [p for p, w in zip((one_back, two_back), PLACES_WITH) if w == (number, axis)]
            for axis in range(2)
        ])

    def before(h, *stages):
        return sum((got[stage][h] for stage in stages), [])

    each("far", False, lambda half, h: send_far(line, half, flat))
    each("raw", False, lambda half, h: send_raw(line, half, flat))
    each("near", False, lambda half, h: send_near(line, half, flat, *before(h, "far")))
    each("far2", True, lambda half, h: send_far2(line, half, flat, before(h, "raw", "near")))
    for number, (first, end) in enumerate(spaces):
        each(
            number, True,
            lambda half, h: send_near2(
                line, half, flat, before(h, "raw", "near"), before(h, "far2"), first // TILE, (end - first) // TILE
            ),
        )
    fresh = update = None
    lists, mine = {}, {}
    for what, number in TAIL:
        number = int(number)
        first, end = spaces[number]
        piece = Part(pair, first, end - first, dict(f=FINE, s=TILE, j=BROAD)[what])
        if what == "f":
            full = [before(h, "raw", "near", number) for h in range(2)]
            fresh, own = finish(line, piece, flat, momentum, positions, full, tables, fresh)
            lists[number] = [own] + [along_z(own, step) for step in (1, -1, 2)]
        elif what == "s":
            part = spread(line, piece, lists[number], places, tables[1])
            mine[number] = part, other_core(part)
        else:
            update = join(line, piece, *mine[number], spans, update)
    return update, fresh


def solution(mesh):
    placed = (P("rep", "fsdp", None, None), P("rep", None, "fsdp"), P("rep", None, "fsdp"))
    return jax.shard_map(
        on_device,
        mesh=mesh,
        in_specs=placed,
        out_specs=(P(None, "fsdp"), P("rep", None, "fsdp")),
        check_vma=False,
    )
```

```python
import jax
import jax.numpy as jnp
import ml_dtypes
import numpy as np
from jax import lax
from jax.experimental import pallas as pl
from jax.experimental.pallas import tpu as pltpu
from jax.sharding import PartitionSpec as P

BLOCK = 64
HALF = BLOCK // 2
KEEP = 8
SIDE = 4
TILE = 1024
CHUNK = 256
FINE, BROAD = 1024, 2048
PARTS = (2, 2)
AXES = (0, 0, 1, 1, 1, 0)
LAG = (2, 2, 2, 2, 2, 2)
PLACES_WITH = ((1, 0), (1, 0))
TAIL = ('f0', 'f1', 's0', 's1', 'j0', 'j1')
TOGETHER = 2
VMEM_LIMIT = 62 * 1024 * 1024
F32 = jnp.float32
BF16 = jnp.bfloat16


def dct_parts():
    k = np.arange(BLOCK, dtype=np.float64)[:, None]
    n = np.arange(BLOCK, dtype=np.float64)[None, :]
    scale = np.where(k == 0, np.sqrt(1.0 / BLOCK), np.sqrt(2.0 / BLOCK))
    dct = scale * np.cos(np.pi * (2.0 * n + 1.0) * k / (2.0 * BLOCK))

    def wide(mat):
        high = mat.astype(ml_dtypes.bfloat16)
        low = (mat - high.astype(np.float64)).astype(ml_dtypes.bfloat16)
        return np.concatenate([high, high, low, low], axis=1)

    return wide(dct), wide(dct.T.copy())


def fold(coord, step):
    return lax.rem(coord + (step + SIDE), SIDE)


class Half:
    def __init__(self, x_first, start, width, spans):
        self.x_first = x_first
        self.width = width
        self.count = width // TILE
        self.first = start // TILE
        self.per_target = spans // TILE

    def column(self, here, step, other):
        y, x = here[0], here[1]
        if self.x_first:
            target = other * SIDE + fold(x, step)
        else:
            target = fold(y, step) * SIDE + other
        return target * self.per_target + self.first

    def second(self, here, step):
        return fold(here[0] if self.x_first else here[1], step)

    def grid_blocks(self, step, rows):
        def spec(other, tile):
            return pl.BlockSpec(
                (HALF, TILE),
                lambda i, here: (rows, self.column(here, step, i * TOGETHER + other) + tile),
            )

        return [spec(other, tile) for other in range(TOGETHER) for tile in range(self.count)]

    def one_blocks(self, step):
        def spec(tile):
            return pl.BlockSpec(
                (BLOCK, TILE),
                lambda i, here: (0, self.column(here, 0, self.second(here, step)) + tile),
            )

        return [spec(tile) for tile in range(self.count)]

    def message_blocks(self, step):
        def spec(tile):
            return pl.BlockSpec(
                (HALF, TILE), lambda i, here: (0, self.second(here, step) * self.count + tile)
            )

        return [spec(tile) for tile in range(self.count)]


def whole(*shape):
    return pl.BlockSpec(shape, lambda i, here: (0,) * len(shape))


class Line:
    def __init__(self, here):
        self.here = here
        self.token = None
        self.arrived = []

    def call(self, body, grid, ins, in_specs, out_shape, out_specs, aliases=None):
        ins, in_specs = list(ins), list(in_specs)
        count = len(ins)
        order = ([] if self.token is None else [self.token]) + self.arrived
        taken = len(order)
        ins += order
        in_specs += [whole(*(1,) * (array.ndim - 2), 8, 128) for array in order]

        def run(here, *refs):
            refs[-1][...] = jnp.zeros((8, 128), F32)
            body(here, *refs[:count], *refs[count + taken : -1])

        *outs, self.token = pl.pallas_call(
            run,
            grid_spec=pltpu.PrefetchScalarGridSpec(
                num_scalar_prefetch=1,
                grid=(grid,),
                in_specs=in_specs,
                out_specs=(*out_specs, whole(8, 128)),
            ),
            out_shape=(*out_shape, jax.ShapeDtypeStruct((8, 128), F32)),
            input_output_aliases=aliases or {},
            compiler_params=pltpu.CompilerParams(vmem_limit_bytes=VMEM_LIMIT),
            cost_estimate=pl.CostEstimate(flops=0, bytes_accessed=0, transcendentals=0),
        )(self.here, *ins)
        return outs


def tiles(n, *groups):
    for tile in range(n):
        yield slice(tile * TILE, (tile + 1) * TILE), [group[tile] for group in groups]


def groups(refs, n):
    return [refs[k : k + n] for k in range(0, len(refs), n)]


def send_part(line, half, partials, up_from, down_from):
    n = half.count * TOGETHER

    def body(here, *refs):
        up, down = refs[2 * n :]
        for col, (part_up, part_down) in tiles(n, *groups(refs[: 2 * n], n)):
            up[:, col] = part_up[...].astype(F32)
            down[:, col] = part_down[...].astype(F32)

    shape = jax.ShapeDtypeStruct((HALF, SIDE * half.width), F32)
    spec = pl.BlockSpec((HALF, n * TILE), lambda i, here: (0, i))
    return line.call(
        body, SIDE // TOGETHER, [partials] * (2 * n),
        half.grid_blocks(*up_from) + half.grid_blocks(*down_from), (shape, shape), (spec, spec),
    )


def send_far(line, half, partials):
    return send_part(line, half, partials, (2, 0), (2, 1))


def send_raw(line, half, partials):
    return send_part(line, half, partials, (1, 1), (-1, 0))


def send_near(line, half, partials, far_up, far_down):
    n = half.count * TOGETHER

    def body(here, *refs):
        far_up, far_down, up, down = refs[2 * n :]
        for col, (part_up, part_down) in tiles(n, *groups(refs[: 2 * n], n)):
            up[:, col] = part_up[...].astype(F32) + far_up[:, col]
            down[:, col] = part_down[...].astype(F32) + far_down[:, col]

    shape = jax.ShapeDtypeStruct((HALF, SIDE * half.width), F32)
    spec = pl.BlockSpec((HALF, n * TILE), lambda i, here: (0, i))
    return line.call(
        body, SIDE // TOGETHER, [partials] * (2 * n) + [far_up, far_down],
        half.grid_blocks(1, 0) + half.grid_blocks(-1, 1) + [spec, spec],
        (shape, shape), (spec, spec),
    )


def repeat(arrays, n):
    return [array for array in arrays for _ in range(n)]


def high_low(part, raw_up, raw_down, near_up, near_down):
    high = part[:HALF].astype(F32) + near_up[...] + raw_down[...]
    low = part[HALF:].astype(F32) + near_down[...] + raw_up[...]
    return high, low


def send_far2(line, half, partials, got):
    w, n = half.width, half.count

    def body(here, *refs):
        up, down = refs[-2:]
        for col, blocks in tiles(n, *groups(refs[: 5 * n], n)):
            up[:, col], down[:, col] = high_low(*blocks)

    shape = jax.ShapeDtypeStruct((HALF, w), F32)
    return line.call(
        body, 1, [partials] * n + repeat(got, n), half.one_blocks(2) + half.message_blocks(2) * 4,
        (shape, shape), (whole(HALF, w), whole(HALF, w)),
    )


def send_near2(line, half, partials, got, far, first, n):
    own = slice(first, first + n)

    def body(here, *refs):
        up, down = refs[-2:]
        for col, blocks in tiles(n, *groups(refs[: 12 * n], n)):
            high, low = high_low(*blocks[:5])
            up[:HALF, col] = high + blocks[10][...]
            up[HALF:, col] = low
            high, low = high_low(*blocks[5:10])
            down[:HALF, col] = high
            down[HALF:, col] = low + blocks[11][...]

    far_specs = [pl.BlockSpec((HALF, TILE), lambda i, here, t=t: (0, t)) for t in range(half.count)]
    w = n * TILE
    shape = jax.ShapeDtypeStruct((BLOCK, w), F32)
    return line.call(
        body, 1, ([partials] * n + repeat(got, n)) * 2 + repeat(far, n),
        half.one_blocks(1)[own] + half.message_blocks(1)[own] * 4 + half.one_blocks(-1)[own]
        + half.message_blocks(-1)[own] * 4 + far_specs[own] * 2,
        (shape, shape), (whole(BLOCK, w), whole(BLOCK, w)),
    )


def product(parts, value):
    high = value.astype(BF16)
    low = (value - high.astype(F32)).astype(BF16)
    return jnp.dot(
        parts[...], jnp.concatenate([high, low, high, low], axis=0), preferred_element_type=F32
    )


def settle(grad_of, momentum, positions, forward, backward, fresh, values):
    for at in range(0, fresh.shape[2], CHUNK):
        col = slice(at, at + CHUNK)
        moment = 0.9 * momentum[0, :, col] + grad_of(col)
        coeff = product(forward, moment)
        chosen = positions[0, :, col]
        freq = lax.broadcasted_iota(jnp.int32, coeff.shape, 0)
        own = jnp.zeros_like(coeff)
        rows = []
        for place in range(KEEP):
            hit = jnp.where(chosen[place : place + 1] == freq, coeff, 0.0)
            rows.append(jnp.sum(hit, axis=0, keepdims=True))
            own = own + hit
        values[:, col] = jnp.concatenate(rows, axis=0)
        fresh[0, :, col] = moment - product(backward, own)


class Part:
    def __init__(self, pair, first, width, tile):
        self.pair, self.tile = pair, tile
        self.first, self.n, self.count = first // tile, width // tile, pair[0].width // tile
        self.steps, self.spans = 2 * self.n, 2 * width

    def place(self, i):
        return jnp.where(i < self.n, i, i - self.n + self.count) + self.first

    def columns(self, rows, block=0):
        return pl.BlockSpec((1, rows, self.tile), lambda i, here: (0, block, self.place(i)))

    def result(self):
        return pl.BlockSpec((BLOCK, self.tile), lambda i, here: (0, self.place(i)))

    def compact(self, rows):
        return pl.BlockSpec((rows, self.tile), lambda i, here: (0, i))


def finish(line, piece, partials, momentum, positions, got, tables, so_far):
    n = piece.n
    ins, specs = [], []
    for number, (half, arrays) in enumerate(zip(piece.pair, got)):
        ins += [partials, *arrays]

        def tile(i, number=number):
            return jnp.minimum(i, n - 1) if number == 0 else jnp.maximum(i - n, 0)

        def part(i, here, half=half, tile=tile):
            target = half.column(here, 0, half.second(here, 0)) * (TILE // piece.tile)
            return 0, target + piece.first + tile(i)

        def message(i, here, half=half, tile=tile):
            return 0, half.second(here, 0) * piece.count + piece.first + tile(i)

        def flat(i, here, tile=tile):
            return 0, tile(i)

        specs += [pl.BlockSpec((BLOCK, piece.tile), part)]
        specs += [pl.BlockSpec((HALF, piece.tile), message)] * 4
        specs += [pl.BlockSpec((BLOCK, piece.tile), flat)] * 2
    ins += [momentum, positions, *tables]
    specs += [piece.columns(BLOCK), piece.columns(KEEP)] + [whole(BLOCK, 4 * BLOCK)] * 2
    aliases = {}
    if so_far is not None:
        ins.append(so_far)
        specs.append(pl.BlockSpec(memory_space=pl.ANY))
        aliases = {len(ins): 0}

    def body(here, *refs):
        momentum, positions, forward, backward = refs[14:18]

        def half(part, raw_up, raw_down, near_up, near_down, left2, right2):
            def grad_of(col):
                first = (raw_up, raw_down, near_up, near_down)
                pair = high_low(part[:, col], *(ref[:, col] for ref in first))
                return jnp.concatenate(pair, axis=0) + left2[:, col] + right2[:, col]

            settle(grad_of, momentum, positions, forward, backward, *refs[-2:])

        @pl.when(pl.program_id(0) < n)
        def _():
            half(*refs[0:7])

        @pl.when(pl.program_id(0) >= n)
        def _():
            half(*refs[7:14])

    return line.call(
        body, piece.steps, ins, specs,
        (jax.ShapeDtypeStruct(momentum.shape, F32), jax.ShapeDtypeStruct((KEEP, piece.spans), F32)),
        (piece.columns(BLOCK), piece.compact(KEEP)), aliases=aliases,
    )


def dense(values, chosen):
    freq = lax.broadcasted_iota(jnp.int32, (BLOCK, values.shape[1]), 0)
    acc = jnp.zeros((BLOCK, values.shape[1]), F32)
    for place in range(KEEP):
        acc = jnp.where(chosen[place : place + 1] == freq, values[place : place + 1], acc)
    return acc


def spread(line, piece, lists, places, table):
    def body(here, *refs):
        backward, out = refs[-2:]
        for at in range(0, piece.tile, CHUNK):
            col = slice(at, at + CHUNK)
            parts = [dense(refs[k][:, col], refs[4 + k][0, :, col]) for k in range(4)]
            out[:, col] = product(backward, (parts[0] + parts[3]) + (parts[1] + parts[2]))

    return line.call(
        body, piece.steps, [*lists, *(array for array, _ in places), table],
        [piece.compact(KEEP)] * 4 + [piece.columns(KEEP, block) for _, block in places]
        + [whole(BLOCK, 4 * BLOCK)],
        (jax.ShapeDtypeStruct((BLOCK, piece.spans), F32),), (piece.compact(BLOCK),),
    )[0]


def join(line, piece, mine, other, spans, so_far):
    ins, specs, aliases = [mine, other], [piece.compact(BLOCK)] * 2, {}
    if so_far is not None:
        ins.append(so_far)
        specs.append(pl.BlockSpec(memory_space=pl.ANY))
        aliases = {3: 0}

    def body(here, *refs):
        refs[-1][...] = refs[0][...] + refs[1][...]

    return line.call(
        body, piece.steps, ins, specs, (jax.ShapeDtypeStruct((BLOCK, spans), F32),),
        (piece.result(),), aliases=aliases,
    )[0]


def shift(dy, dx):
    return [
        (y * SIDE + x, (y + dy) % SIDE * SIDE + (x + dx) % SIDE)
        for y in range(SIDE)
        for x in range(SIDE)
    ]


def along(x_first, value, step):
    return lax.ppermute(value, "fsdp", shift(0, step) if x_first else shift(step, 0))


def along_z(value, step):
    return lax.ppermute(
        value, "rep", [(z * 2 + c, (z + step) % SIDE * 2 + c) for z in range(SIDE) for c in range(2)]
    )


def other_core(value):
    return lax.ppermute(value, "rep", [(r, r ^ 1) for r in range(2 * SIDE)])


def both(x_first, sent):
    return [along(x_first, sent[0], 1), along(x_first, sent[1], -1)]


def on_device(partials, momentum, positions):
    spans = momentum.shape[2]
    flat = partials.reshape(partials.shape[2:])
    me = lax.axis_index("fsdp")
    here = jnp.stack([me // SIDE, lax.rem(me, SIDE)]).astype(jnp.int32)
    tables = tuple(jnp.asarray(part) for part in dct_parts())
    line = Line(here)
    one_back = along_z(positions, 1)
    two_back = along_z(jnp.concatenate([positions, one_back], axis=1), 2)
    places = [(positions, 0), (one_back, 0), (two_back, 1), (two_back, 0)]
    width = spans // 2
    pair = (Half(True, 0, width, spans), Half(False, width, width, spans))
    ends = [TILE * sum(PARTS[:number]) for number in range(len(PARTS) + 1)]
    spaces = list(zip(ends, ends[1:]))
    got, sent = {}, []

    def each(stage, second, send):
        number = len(sent)
        out = [None, None]
        for axis in (AXES[number], 1 - AXES[number]):
            h = 1 - axis if second else axis
            line.arrived = sent[number - LAG[number]][axis] if number >= LAG[number] else []
            out[h] = both(axis == 0, send(pair[h], h))
        line.arrived = []
        got[stage] = out
        messages = out[::-1] if second else out
        sent.append([
            messages[axis] + [p for p, w in zip((one_back, two_back), PLACES_WITH) if w == (number, axis)]
            for axis in range(2)
        ])

    def before(h, *stages):
        return sum((got[stage][h] for stage in stages), [])

    each("far", False, lambda half, h: send_far(line, half, flat))
    each("raw", False, lambda half, h: send_raw(line, half, flat))
    each("near", False, lambda half, h: send_near(line, half, flat, *before(h, "far")))
    each("far2", True, lambda half, h: send_far2(line, half, flat, before(h, "raw", "near")))
    for number, (first, end) in enumerate(spaces):
        each(
            number, True,
            lambda half, h: send_near2(
                line, half, flat, before(h, "raw", "near"), before(h, "far2"), first // TILE, (end - first) // TILE
            ),
        )
    fresh = update = None
    lists, mine = {}, {}
    for what, number in TAIL:
        number = int(number)
        first, end = spaces[number]
        piece = Part(pair, first, end - first, dict(f=FINE, s=TILE, j=BROAD)[what])
        if what == "f":
            full = [before(h, "raw", "near", number) for h in range(2)]
            fresh, own = finish(line, piece, flat, momentum, positions, full, tables, fresh)
            lists[number] = [own] + [along_z(own, step) for step in (1, -1, 2)]
        elif what == "s":
            part = spread(line, piece, lists[number], places, tables[1])
            mine[number] = part, other_core(part)
        else:
            update = join(line, piece, *mine[number], spans, update)
    return update, fresh


def solution(mesh):
    placed = (P("rep", "fsdp", None, None), P("rep", None, "fsdp"), P("rep", None, "fsdp"))
    return jax.shard_map(
        on_device,
        mesh=mesh,
        in_specs=placed,
        out_specs=(P(None, "fsdp"), P("rep", None, "fsdp")),
        check_vma=False,
    )
```

```python
import jax
import jax.numpy as jnp
import ml_dtypes
import numpy as np
from jax import lax
from jax.experimental import pallas as pl
from jax.experimental.pallas import tpu as pltpu
from jax.sharding import PartitionSpec as P

BLOCK = 64
HALF = BLOCK // 2
KEEP = 8
SIDE = 4
TILE = 1024
CHUNK = 256
FINE, BROAD = 1024, 2048
PARTS = (2, 2)
AXES = (0, 0, 1, 1, 1, 0)
LAG = (2, 2, 2, 2, 2, 2)
PLACES_WITH = ((1, 0), (1, 0))
TAIL = ('f0', 'f1', 's0', 's1', 'j0', 'j1')
TOGETHER = 2
VMEM_LIMIT = 48 * 1024 * 1024
F32 = jnp.float32
BF16 = jnp.bfloat16


def dct_parts():
    k = np.arange(BLOCK, dtype=np.float64)[:, None]
    n = np.arange(BLOCK, dtype=np.float64)[None, :]
    scale = np.where(k == 0, np.sqrt(1.0 / BLOCK), np.sqrt(2.0 / BLOCK))
    dct = scale * np.cos(np.pi * (2.0 * n + 1.0) * k / (2.0 * BLOCK))

    def wide(mat):
        high = mat.astype(ml_dtypes.bfloat16)
        low = (mat - high.astype(np.float64)).astype(ml_dtypes.bfloat16)
        return np.concatenate([high, high, low, low], axis=1)

    return wide(dct), wide(dct.T.copy())


def fold(coord, step):
    return lax.rem(coord + (step + SIDE), SIDE)


class Half:
    def __init__(self, x_first, start, width, spans):
        self.x_first = x_first
        self.width = width
        self.count = width // TILE
        self.first = start // TILE
        self.per_target = spans // TILE

    def column(self, here, step, other):
        y, x = here[0], here[1]
        if self.x_first:
            target = other * SIDE + fold(x, step)
        else:
            target = fold(y, step) * SIDE + other
        return target * self.per_target + self.first

    def second(self, here, step):
        return fold(here[0] if self.x_first else here[1], step)

    def grid_blocks(self, step, rows):
        def spec(other, tile):
            return pl.BlockSpec(
                (HALF, TILE),
                lambda i, here: (rows, self.column(here, step, i * TOGETHER + other) + tile),
            )

        return [spec(other, tile) for other in range(TOGETHER) for tile in range(self.count)]

    def one_blocks(self, step):
        def spec(tile):
            return pl.BlockSpec(
                (BLOCK, TILE),
                lambda i, here: (0, self.column(here, 0, self.second(here, step)) + tile),
            )

        return [spec(tile) for tile in range(self.count)]

    def message_blocks(self, step):
        def spec(tile):
            return pl.BlockSpec(
                (HALF, TILE), lambda i, here: (0, self.second(here, step) * self.count + tile)
            )

        return [spec(tile) for tile in range(self.count)]


def whole(*shape):
    return pl.BlockSpec(shape, lambda i, here: (0,) * len(shape))


class Line:
    def __init__(self, here):
        self.here = here
        self.token = None
        self.arrived = []

    def call(self, body, grid, ins, in_specs, out_shape, out_specs, aliases=None):
        ins, in_specs = list(ins), list(in_specs)
        count = len(ins)
        order = ([] if self.token is None else [self.token]) + self.arrived
        taken = len(order)
        ins += order
        in_specs += [whole(*(1,) * (array.ndim - 2), 8, 128) for array in order]

        def run(here, *refs):
            refs[-1][...] = jnp.zeros((8, 128), F32)
            body(here, *refs[:count], *refs[count + taken : -1])

        *outs, self.token = pl.pallas_call(
            run,
            grid_spec=pltpu.PrefetchScalarGridSpec(
                num_scalar_prefetch=1,
                grid=(grid,),
                in_specs=in_specs,
                out_specs=(*out_specs, whole(8, 128)),
            ),
            out_shape=(*out_shape, jax.ShapeDtypeStruct((8, 128), F32)),
            input_output_aliases=aliases or {},
            compiler_params=pltpu.CompilerParams(vmem_limit_bytes=VMEM_LIMIT),
            cost_estimate=pl.CostEstimate(flops=0, bytes_accessed=0, transcendentals=0),
        )(self.here, *ins)
        return outs


def tiles(n, *groups):
    for tile in range(n):
        yield slice(tile * TILE, (tile + 1) * TILE), [group[tile] for group in groups]


def groups(refs, n):
    return [refs[k : k + n] for k in range(0, len(refs), n)]


def send_part(line, half, partials, up_from, down_from):
    n = half.count * TOGETHER

    def body(here, *refs):
        up, down = refs[2 * n :]
        for col, (part_up, part_down) in tiles(n, *groups(refs[: 2 * n], n)):
            up[:, col] = part_up[...].astype(F32)
            down[:, col] = part_down[...].astype(F32)

    shape = jax.ShapeDtypeStruct((HALF, SIDE * half.width), F32)
    spec = pl.BlockSpec((HALF, n * TILE), lambda i, here: (0, i))
    return line.call(
        body, SIDE // TOGETHER, [partials] * (2 * n),
        half.grid_blocks(*up_from) + half.grid_blocks(*down_from), (shape, shape), (spec, spec),
    )


def send_far(line, half, partials):
    return send_part(line, half, partials, (2, 0), (2, 1))


def send_raw(line, half, partials):
    return send_part(line, half, partials, (1, 1), (-1, 0))


def send_near(line, half, partials, far_up, far_down):
    n = half.count * TOGETHER

    def body(here, *refs):
        far_up, far_down, up, down = refs[2 * n :]
        for col, (part_up, part_down) in tiles(n, *groups(refs[: 2 * n], n)):
            up[:, col] = part_up[...].astype(F32) + far_up[:, col]
            down[:, col] = part_down[...].astype(F32) + far_down[:, col]

    shape = jax.ShapeDtypeStruct((HALF, SIDE * half.width), F32)
    spec = pl.BlockSpec((HALF, n * TILE), lambda i, here: (0, i))
    return line.call(
        body, SIDE // TOGETHER, [partials] * (2 * n) + [far_up, far_down],
        half.grid_blocks(1, 0) + half.grid_blocks(-1, 1) + [spec, spec],
        (shape, shape), (spec, spec),
    )


def repeat(arrays, n):
    return [array for array in arrays for _ in range(n)]


def high_low(part, raw_up, raw_down, near_up, near_down):
    high = part[:HALF].astype(F32) + near_up[...] + raw_down[...]
    low = part[HALF:].astype(F32) + near_down[...] + raw_up[...]
    return high, low


def send_far2(line, half, partials, got):
    w, n = half.width, half.count

    def body(here, *refs):
        up, down = refs[-2:]
        for col, blocks in tiles(n, *groups(refs[: 5 * n], n)):
            up[:, col], down[:, col] = high_low(*blocks)

    shape = jax.ShapeDtypeStruct((HALF, w), F32)
    return line.call(
        body, 1, [partials] * n + repeat(got, n), half.one_blocks(2) + half.message_blocks(2) * 4,
        (shape, shape), (whole(HALF, w), whole(HALF, w)),
    )


def send_near2(line, half, partials, got, far, first, n):
    own = slice(first, first + n)

    def body(here, *refs):
        up, down = refs[-2:]
        for col, blocks in tiles(n, *groups(refs[: 12 * n], n)):
            high, low = high_low(*blocks[:5])
            up[:HALF, col] = high + blocks[10][...]
            up[HALF:, col] = low
            high, low = high_low(*blocks[5:10])
            down[:HALF, col] = high
            down[HALF:, col] = low + blocks[11][...]

    far_specs = [pl.BlockSpec((HALF, TILE), lambda i, here, t=t: (0, t)) for t in range(half.count)]
    w = n * TILE
    shape = jax.ShapeDtypeStruct((BLOCK, w), F32)
    return line.call(
        body, 1, ([partials] * n + repeat(got, n)) * 2 + repeat(far, n),
        half.one_blocks(1)[own] + half.message_blocks(1)[own] * 4 + half.one_blocks(-1)[own]
        + half.message_blocks(-1)[own] * 4 + far_specs[own] * 2,
        (shape, shape), (whole(BLOCK, w), whole(BLOCK, w)),
    )


def product(parts, value):
    high = value.astype(BF16)
    low = (value - high.astype(F32)).astype(BF16)
    return jnp.dot(
        parts[...], jnp.concatenate([high, low, high, low], axis=0), preferred_element_type=F32
    )


def settle(grad_of, momentum, positions, forward, backward, fresh, values):
    for at in range(0, fresh.shape[2], CHUNK):
        col = slice(at, at + CHUNK)
        moment = 0.9 * momentum[0, :, col] + grad_of(col)
        coeff = product(forward, moment)
        chosen = positions[0, :, col]
        freq = lax.broadcasted_iota(jnp.int32, coeff.shape, 0)
        own = jnp.zeros_like(coeff)
        rows = []
        for place in range(KEEP):
            hit = jnp.where(chosen[place : place + 1] == freq, coeff, 0.0)
            rows.append(jnp.sum(hit, axis=0, keepdims=True))
            own = own + hit
        values[:, col] = jnp.concatenate(rows, axis=0)
        fresh[0, :, col] = moment - product(backward, own)


class Part:
    def __init__(self, pair, first, width, tile):
        self.pair, self.tile = pair, tile
        self.first, self.n, self.count = first // tile, width // tile, pair[0].width // tile
        self.steps, self.spans = 2 * self.n, 2 * width

    def place(self, i):
        return jnp.where(i < self.n, i, i - self.n + self.count) + self.first

    def columns(self, rows, block=0):
        return pl.BlockSpec((1, rows, self.tile), lambda i, here: (0, block, self.place(i)))

    def result(self):
        return pl.BlockSpec((BLOCK, self.tile), lambda i, here: (0, self.place(i)))

    def compact(self, rows):
        return pl.BlockSpec((rows, self.tile), lambda i, here: (0, i))


def finish(line, piece, partials, momentum, positions, got, tables, so_far):
    n = piece.n
    ins, specs = [], []
    for number, (half, arrays) in enumerate(zip(piece.pair, got)):
        ins += [partials, *arrays]

        def tile(i, number=number):
            return jnp.minimum(i, n - 1) if number == 0 else jnp.maximum(i - n, 0)

        def part(i, here, half=half, tile=tile):
            target = half.column(here, 0, half.second(here, 0)) * (TILE // piece.tile)
            return 0, target + piece.first + tile(i)

        def message(i, here, half=half, tile=tile):
            return 0, half.second(here, 0) * piece.count + piece.first + tile(i)

        def flat(i, here, tile=tile):
            return 0, tile(i)

        specs += [pl.BlockSpec((BLOCK, piece.tile), part)]
        specs += [pl.BlockSpec((HALF, piece.tile), message)] * 4
        specs += [pl.BlockSpec((BLOCK, piece.tile), flat)] * 2
    ins += [momentum, positions, *tables]
    specs += [piece.columns(BLOCK), piece.columns(KEEP)] + [whole(BLOCK, 4 * BLOCK)] * 2
    aliases = {}
    if so_far is not None:
        ins.append(so_far)
        specs.append(pl.BlockSpec(memory_space=pl.ANY))
        aliases = {len(ins): 0}

    def body(here, *refs):
        momentum, positions, forward, backward = refs[14:18]

        def half(part, raw_up, raw_down, near_up, near_down, left2, right2):
            def grad_of(col):
                first = (raw_up, raw_down, near_up, near_down)
                pair = high_low(part[:, col], *(ref[:, col] for ref in first))
                return jnp.concatenate(pair, axis=0) + left2[:, col] + right2[:, col]

            settle(grad_of, momentum, positions, forward, backward, *refs[-2:])

        @pl.when(pl.program_id(0) < n)
        def _():
            half(*refs[0:7])

        @pl.when(pl.program_id(0) >= n)
        def _():
            half(*refs[7:14])

    return line.call(
        body, piece.steps, ins, specs,
        (jax.ShapeDtypeStruct(momentum.shape, F32), jax.ShapeDtypeStruct((KEEP, piece.spans), F32)),
        (piece.columns(BLOCK), piece.compact(KEEP)), aliases=aliases,
    )


def dense(values, chosen):
    freq = lax.broadcasted_iota(jnp.int32, (BLOCK, values.shape[1]), 0)
    acc = jnp.zeros((BLOCK, values.shape[1]), F32)
    for place in range(KEEP):
        acc = jnp.where(chosen[place : place + 1] == freq, values[place : place + 1], acc)
    return acc


def spread(line, piece, lists, places, table):
    def body(here, *refs):
        backward, out = refs[-2:]
        for at in range(0, piece.tile, CHUNK):
            col = slice(at, at + CHUNK)
            parts = [dense(refs[k][:, col], refs[4 + k][0, :, col]) for k in range(4)]
            out[:, col] = product(backward, (parts[0] + parts[3]) + (parts[1] + parts[2]))

    return line.call(
        body, piece.steps, [*lists, *(array for array, _ in places), table],
        [piece.compact(KEEP)] * 4 + [piece.columns(KEEP, block) for _, block in places]
        + [whole(BLOCK, 4 * BLOCK)],
        (jax.ShapeDtypeStruct((BLOCK, piece.spans), F32),), (piece.compact(BLOCK),),
    )[0]


def join(line, piece, mine, other, spans, so_far):
    ins, specs, aliases = [mine, other], [piece.compact(BLOCK)] * 2, {}
    if so_far is not None:
        ins.append(so_far)
        specs.append(pl.BlockSpec(memory_space=pl.ANY))
        aliases = {3: 0}

    def body(here, *refs):
        refs[-1][...] = refs[0][...] + refs[1][...]

    return line.call(
        body, piece.steps, ins, specs, (jax.ShapeDtypeStruct((BLOCK, spans), F32),),
        (piece.result(),), aliases=aliases,
    )[0]


def shift(dy, dx):
    return [
        (y * SIDE + x, (y + dy) % SIDE * SIDE + (x + dx) % SIDE)
        for y in range(SIDE)
        for x in range(SIDE)
    ]


def along(x_first, value, step):
    return lax.ppermute(value, "fsdp", shift(0, step) if x_first else shift(step, 0))


def along_z(value, step):
    return lax.ppermute(
        value, "rep", [(z * 2 + c, (z + step) % SIDE * 2 + c) for z in range(SIDE) for c in range(2)]
    )


def other_core(value):
    return lax.ppermute(value, "rep", [(r, r ^ 1) for r in range(2 * SIDE)])


def both(x_first, sent):
    return [along(x_first, sent[0], 1), along(x_first, sent[1], -1)]


def on_device(partials, momentum, positions):
    spans = momentum.shape[2]
    flat = partials.reshape(partials.shape[2:])
    me = lax.axis_index("fsdp")
    here = jnp.stack([me // SIDE, lax.rem(me, SIDE)]).astype(jnp.int32)
    tables = tuple(jnp.asarray(part) for part in dct_parts())
    line = Line(here)
    one_back = along_z(positions, 1)
    two_back = along_z(jnp.concatenate([positions, one_back], axis=1), 2)
    places = [(positions, 0), (one_back, 0), (two_back, 1), (two_back, 0)]
    width = spans // 2
    pair = (Half(True, 0, width, spans), Half(False, width, width, spans))
    ends = [TILE * sum(PARTS[:number]) for number in range(len(PARTS) + 1)]
    spaces = list(zip(ends, ends[1:]))
    got, sent = {}, []

    def each(stage, second, send):
        number = len(sent)
        out = [None, None]
        for axis in (AXES[number], 1 - AXES[number]):
            h = 1 - axis if second else axis
            line.arrived = sent[number - LAG[number]][axis] if number >= LAG[number] else []
            out[h] = both(axis == 0, send(pair[h], h))
        line.arrived = []
        got[stage] = out
        messages = out[::-1] if second else out
        sent.append([
            messages[axis] + [p for p, w in zip((one_back, two_back), PLACES_WITH) if w == (number, axis)]
            for axis in range(2)
        ])

    def before(h, *stages):
        return sum((got[stage][h] for stage in stages), [])

    each("far", False, lambda half, h: send_far(line, half, flat))
    each("raw", False, lambda half, h: send_raw(line, half, flat))
    each("near", False, lambda half, h: send_near(line, half, flat, *before(h, "far")))
    each("far2", True, lambda half, h: send_far2(line, half, flat, before(h, "raw", "near")))
    for number, (first, end) in enumerate(spaces):
        each(
            number, True,
            lambda half, h: send_near2(
                line, half, flat, before(h, "raw", "near"), before(h, "far2"), first // TILE, (end - first) // TILE
            ),
        )
    fresh = update = None
    lists, mine = {}, {}
    for what, number in TAIL:
        number = int(number)
        first, end = spaces[number]
        piece = Part(pair, first, end - first, dict(f=FINE, s=TILE, j=BROAD)[what])
        if what == "f":
            full = [before(h, "raw", "near", number) for h in range(2)]
            fresh, own = finish(line, piece, flat, momentum, positions, full, tables, fresh)
            lists[number] = [own] + [along_z(own, step) for step in (1, -1, 2)]
        elif what == "s":
            part = spread(line, piece, lists[number], places, tables[1])
            mine[number] = part, other_core(part)
        else:
            update = join(line, piece, *mine[number], spans, update)
    return update, fresh


def solution(mesh):
    placed = (P("rep", "fsdp", None, None), P("rep", None, "fsdp"), P("rep", None, "fsdp"))
    return jax.shard_map(
        on_device,
        mesh=mesh,
        in_specs=placed,
        out_specs=(P(None, "fsdp"), P("rep", None, "fsdp")),
        check_vma=False,
    )
```

```python
import jax
import jax.numpy as jnp
import ml_dtypes
import numpy as np
from jax import lax
from jax.experimental import pallas as pl
from jax.experimental.pallas import tpu as pltpu
from jax.sharding import PartitionSpec as P

BLOCK = 64
HALF = BLOCK // 2
KEEP = 8
SIDE = 4
TILE = 1024
CHUNK = 256
FINE, BROAD = 1024, 2048
PARTS = (2, 2)
AXES = (0, 0, 1, 1, 1, 0)
LAG = (2, 2, 2, 2, 2, 2)
PLACES_WITH = ((1, 0), (1, 0))
TAIL = ('f0', 'f1', 's0', 's1', 'j0', 'j1')
TOGETHER = 2
VMEM_LIMIT = 36 * 1024 * 1024
F32 = jnp.float32
BF16 = jnp.bfloat16


def dct_parts():
    k = np.arange(BLOCK, dtype=np.float64)[:, None]
    n = np.arange(BLOCK, dtype=np.float64)[None, :]
    scale = np.where(k == 0, np.sqrt(1.0 / BLOCK), np.sqrt(2.0 / BLOCK))
    dct = scale * np.cos(np.pi * (2.0 * n + 1.0) * k / (2.0 * BLOCK))

    def wide(mat):
        high = mat.astype(ml_dtypes.bfloat16)
        low = (mat - high.astype(np.float64)).astype(ml_dtypes.bfloat16)
        return np.concatenate([high, high, low, low], axis=1)

    return wide(dct), wide(dct.T.copy())


def fold(coord, step):
    return lax.rem(coord + (step + SIDE), SIDE)


class Half:
    def __init__(self, x_first, start, width, spans):
        self.x_first = x_first
        self.width = width
        self.count = width // TILE
        self.first = start // TILE
        self.per_target = spans // TILE

    def column(self, here, step, other):
        y, x = here[0], here[1]
        if self.x_first:
            target = other * SIDE + fold(x, step)
        else:
            target = fold(y, step) * SIDE + other
        return target * self.per_target + self.first

    def second(self, here, step):
        return fold(here[0] if self.x_first else here[1], step)

    def grid_blocks(self, step, rows):
        def spec(other, tile):
            return pl.BlockSpec(
                (HALF, TILE),
                lambda i, here: (rows, self.column(here, step, i * TOGETHER + other) + tile),
            )

        return [spec(other, tile) for other in range(TOGETHER) for tile in range(self.count)]

    def one_blocks(self, step):
        def spec(tile):
            return pl.BlockSpec(
                (BLOCK, TILE),
                lambda i, here: (0, self.column(here, 0, self.second(here, step)) + tile),
            )

        return [spec(tile) for tile in range(self.count)]

    def message_blocks(self, step):
        def spec(tile):
            return pl.BlockSpec(
                (HALF, TILE), lambda i, here: (0, self.second(here, step) * self.count + tile)
            )

        return [spec(tile) for tile in range(self.count)]


def whole(*shape):
    return pl.BlockSpec(shape, lambda i, here: (0,) * len(shape))


class Line:
    def __init__(self, here):
        self.here = here
        self.token = None
        self.arrived = []

    def call(self, body, grid, ins, in_specs, out_shape, out_specs, aliases=None):
        ins, in_specs = list(ins), list(in_specs)
        count = len(ins)
        order = ([] if self.token is None else [self.token]) + self.arrived
        taken = len(order)
        ins += order
        in_specs += [whole(*(1,) * (array.ndim - 2), 8, 128) for array in order]

        def run(here, *refs):
            refs[-1][...] = jnp.zeros((8, 128), F32)
            body(here, *refs[:count], *refs[count + taken : -1])

        *outs, self.token = pl.pallas_call(
            run,
            grid_spec=pltpu.PrefetchScalarGridSpec(
                num_scalar_prefetch=1,
                grid=(grid,),
                in_specs=in_specs,
                out_specs=(*out_specs, whole(8, 128)),
            ),
            out_shape=(*out_shape, jax.ShapeDtypeStruct((8, 128), F32)),
            input_output_aliases=aliases or {},
            compiler_params=pltpu.CompilerParams(vmem_limit_bytes=VMEM_LIMIT),
            cost_estimate=pl.CostEstimate(flops=0, bytes_accessed=0, transcendentals=0),
        )(self.here, *ins)
        return outs


def tiles(n, *groups):
    for tile in range(n):
        yield slice(tile * TILE, (tile + 1) * TILE), [group[tile] for group in groups]


def groups(refs, n):
    return [refs[k : k + n] for k in range(0, len(refs), n)]


def send_part(line, half, partials, up_from, down_from):
    n = half.count * TOGETHER

    def body(here, *refs):
        up, down = refs[2 * n :]
        for col, (part_up, part_down) in tiles(n, *groups(refs[: 2 * n], n)):
            up[:, col] = part_up[...].astype(F32)
            down[:, col] = part_down[...].astype(F32)

    shape = jax.ShapeDtypeStruct((HALF, SIDE * half.width), F32)
    spec = pl.BlockSpec((HALF, n * TILE), lambda i, here: (0, i))
    return line.call(
        body, SIDE // TOGETHER, [partials] * (2 * n),
        half.grid_blocks(*up_from) + half.grid_blocks(*down_from), (shape, shape), (spec, spec),
    )


def send_far(line, half, partials):
    return send_part(line, half, partials, (2, 0), (2, 1))


def send_raw(line, half, partials):
    return send_part(line, half, partials, (1, 1), (-1, 0))


def send_near(line, half, partials, far_up, far_down):
    n = half.count * TOGETHER

    def body(here, *refs):
        far_up, far_down, up, down = refs[2 * n :]
        for col, (part_up, part_down) in tiles(n, *groups(refs[: 2 * n], n)):
            up[:, col] = part_up[...].astype(F32) + far_up[:, col]
            down[:, col] = part_down[...].astype(F32) + far_down[:, col]

    shape = jax.ShapeDtypeStruct((HALF, SIDE * half.width), F32)
    spec = pl.BlockSpec((HALF, n * TILE), lambda i, here: (0, i))
    return line.call(
        body, SIDE // TOGETHER, [partials] * (2 * n) + [far_up, far_down],
        half.grid_blocks(1, 0) + half.grid_blocks(-1, 1) + [spec, spec],
        (shape, shape), (spec, spec),
    )


def repeat(arrays, n):
    return [array for array in arrays for _ in range(n)]


def high_low(part, raw_up, raw_down, near_up, near_down):
    high = part[:HALF].astype(F32) + near_up[...] + raw_down[...]
    low = part[HALF:].astype(F32) + near_down[...] + raw_up[...]
    return high, low


def send_far2(line, half, partials, got):
    w, n = half.width, half.count

    def body(here, *refs):
        up, down = refs[-2:]
        for col, blocks in tiles(n, *groups(refs[: 5 * n], n)):
            up[:, col], down[:, col] = high_low(*blocks)

    shape = jax.ShapeDtypeStruct((HALF, w), F32)
    return line.call(
        body, 1, [partials] * n + repeat(got, n), half.one_blocks(2) + half.message_blocks(2) * 4,
        (shape, shape), (whole(HALF, w), whole(HALF, w)),
    )


def send_near2(line, half, partials, got, far, first, n):
    own = slice(first, first + n)

    def body(here, *refs):
        up, down = refs[-2:]
        for col, blocks in tiles(n, *groups(refs[: 12 * n], n)):
            high, low = high_low(*blocks[:5])
            up[:HALF, col] = high + blocks[10][...]
            up[HALF:, col] = low
            high, low = high_low(*blocks[5:10])
            down[:HALF, col] = high
            down[HALF:, col] = low + blocks[11][...]

    far_specs = [pl.BlockSpec((HALF, TILE), lambda i, here, t=t: (0, t)) for t in range(half.count)]
    w = n * TILE
    shape = jax.ShapeDtypeStruct((BLOCK, w), F32)
    return line.call(
        body, 1, ([partials] * n + repeat(got, n)) * 2 + repeat(far, n),
        half.one_blocks(1)[own] + half.message_blocks(1)[own] * 4 + half.one_blocks(-1)[own]
        + half.message_blocks(-1)[own] * 4 + far_specs[own] * 2,
        (shape, shape), (whole(BLOCK, w), whole(BLOCK, w)),
    )


def product(parts, value):
    high = value.astype(BF16)
    low = (value - high.astype(F32)).astype(BF16)
    return jnp.dot(
        parts[...], jnp.concatenate([high, low, high, low], axis=0), preferred_element_type=F32
    )


def settle(grad_of, momentum, positions, forward, backward, fresh, values):
    for at in range(0, fresh.shape[2], CHUNK):
        col = slice(at, at + CHUNK)
        moment = 0.9 * momentum[0, :, col] + grad_of(col)
        coeff = product(forward, moment)
        chosen = positions[0, :, col]
        freq = lax.broadcasted_iota(jnp.int32, coeff.shape, 0)
        own = jnp.zeros_like(coeff)
        rows = []
        for place in range(KEEP):
            hit = jnp.where(chosen[place : place + 1] == freq, coeff, 0.0)
            rows.append(jnp.sum(hit, axis=0, keepdims=True))
            own = own + hit
        values[:, col] = jnp.concatenate(rows, axis=0)
        fresh[0, :, col] = moment - product(backward, own)


class Part:
    def __init__(self, pair, first, width, tile):
        self.pair, self.tile = pair, tile
        self.first, self.n, self.count = first // tile, width // tile, pair[0].width // tile
        self.steps, self.spans = 2 * self.n, 2 * width

    def place(self, i):
        return jnp.where(i < self.n, i, i - self.n + self.count) + self.first

    def columns(self, rows, block=0):
        return pl.BlockSpec((1, rows, self.tile), lambda i, here: (0, block, self.place(i)))

    def result(self):
        return pl.BlockSpec((BLOCK, self.tile), lambda i, here: (0, self.place(i)))

    def compact(self, rows):
        return pl.BlockSpec((rows, self.tile), lambda i, here: (0, i))


def finish(line, piece, partials, momentum, positions, got, tables, so_far):
    n = piece.n
    ins, specs = [], []
    for number, (half, arrays) in enumerate(zip(piece.pair, got)):
        ins += [partials, *arrays]

        def tile(i, number=number):
            return jnp.minimum(i, n - 1) if number == 0 else jnp.maximum(i - n, 0)

        def part(i, here, half=half, tile=tile):
            target = half.column(here, 0, half.second(here, 0)) * (TILE // piece.tile)
            return 0, target + piece.first + tile(i)

        def message(i, here, half=half, tile=tile):
            return 0, half.second(here, 0) * piece.count + piece.first + tile(i)

        def flat(i, here, tile=tile):
            return 0, tile(i)

        specs += [pl.BlockSpec((BLOCK, piece.tile), part)]
        specs += [pl.BlockSpec((HALF, piece.tile), message)] * 4
        specs += [pl.BlockSpec((BLOCK, piece.tile), flat)] * 2
    ins += [momentum, positions, *tables]
    specs += [piece.columns(BLOCK), piece.columns(KEEP)] + [whole(BLOCK, 4 * BLOCK)] * 2
    aliases = {}
    if so_far is not None:
        ins.append(so_far)
        specs.append(pl.BlockSpec(memory_space=pl.ANY))
        aliases = {len(ins): 0}

    def body(here, *refs):
        momentum, positions, forward, backward = refs[14:18]

        def half(part, raw_up, raw_down, near_up, near_down, left2, right2):
            def grad_of(col):
                first = (raw_up, raw_down, near_up, near_down)
                pair = high_low(part[:, col], *(ref[:, col] for ref in first))
                return jnp.concatenate(pair, axis=0) + left2[:, col] + right2[:, col]

            settle(grad_of, momentum, positions, forward, backward, *refs[-2:])

        @pl.when(pl.program_id(0) < n)
        def _():
            half(*refs[0:7])

        @pl.when(pl.program_id(0) >= n)
        def _():
            half(*refs[7:14])

    return line.call(
        body, piece.steps, ins, specs,
        (jax.ShapeDtypeStruct(momentum.shape, F32), jax.ShapeDtypeStruct((KEEP, piece.spans), F32)),
        (piece.columns(BLOCK), piece.compact(KEEP)), aliases=aliases,
    )


def dense(values, chosen):
    freq = lax.broadcasted_iota(jnp.int32, (BLOCK, values.shape[1]), 0)
    acc = jnp.zeros((BLOCK, values.shape[1]), F32)
    for place in range(KEEP):
        acc = jnp.where(chosen[place : place + 1] == freq, values[place : place + 1], acc)
    return acc


def spread(line, piece, lists, places, table):
    def body(here, *refs):
        backward, out = refs[-2:]
        for at in range(0, piece.tile, CHUNK):
            col = slice(at, at + CHUNK)
            parts = [dense(refs[k][:, col], refs[4 + k][0, :, col]) for k in range(4)]
            out[:, col] = product(backward, (parts[0] + parts[3]) + (parts[1] + parts[2]))

    return line.call(
        body, piece.steps, [*lists, *(array for array, _ in places), table],
        [piece.compact(KEEP)] * 4 + [piece.columns(KEEP, block) for _, block in places]
        + [whole(BLOCK, 4 * BLOCK)],
        (jax.ShapeDtypeStruct((BLOCK, piece.spans), F32),), (piece.compact(BLOCK),),
    )[0]


def join(line, piece, mine, other, spans, so_far):
    ins, specs, aliases = [mine, other], [piece.compact(BLOCK)] * 2, {}
    if so_far is not None:
        ins.append(so_far)
        specs.append(pl.BlockSpec(memory_space=pl.ANY))
        aliases = {3: 0}

    def body(here, *refs):
        refs[-1][...] = refs[0][...] + refs[1][...]

    return line.call(
        body, piece.steps, ins, specs, (jax.ShapeDtypeStruct((BLOCK, spans), F32),),
        (piece.result(),), aliases=aliases,
    )[0]


def shift(dy, dx):
    return [
        (y * SIDE + x, (y + dy) % SIDE * SIDE + (x + dx) % SIDE)
        for y in range(SIDE)
        for x in range(SIDE)
    ]


def along(x_first, value, step):
    return lax.ppermute(value, "fsdp", shift(0, step) if x_first else shift(step, 0))


def along_z(value, step):
    return lax.ppermute(
        value, "rep", [(z * 2 + c, (z + step) % SIDE * 2 + c) for z in range(SIDE) for c in range(2)]
    )


def other_core(value):
    return lax.ppermute(value, "rep", [(r, r ^ 1) for r in range(2 * SIDE)])


def both(x_first, sent):
    return [along(x_first, sent[0], 1), along(x_first, sent[1], -1)]


def on_device(partials, momentum, positions):
    spans = momentum.shape[2]
    flat = partials.reshape(partials.shape[2:])
    me = lax.axis_index("fsdp")
    here = jnp.stack([me // SIDE, lax.rem(me, SIDE)]).astype(jnp.int32)
    tables = tuple(jnp.asarray(part) for part in dct_parts())
    line = Line(here)
    one_back = along_z(positions, 1)
    two_back = along_z(jnp.concatenate([positions, one_back], axis=1), 2)
    places = [(positions, 0), (one_back, 0), (two_back, 1), (two_back, 0)]
    width = spans // 2
    pair = (Half(True, 0, width, spans), Half(False, width, width, spans))
    ends = [TILE * sum(PARTS[:number]) for number in range(len(PARTS) + 1)]
    spaces = list(zip(ends, ends[1:]))
    got, sent = {}, []

    def each(stage, second, send):
        number = len(sent)
        out = [None, None]
        for axis in (AXES[number], 1 - AXES[number]):
            h = 1 - axis if second else axis
            line.arrived = sent[number - LAG[number]][axis] if number >= LAG[number] else []
            out[h] = both(axis == 0, send(pair[h], h))
        line.arrived = []
        got[stage] = out
        messages = out[::-1] if second else out
        sent.append([
            messages[axis] + [p for p, w in zip((one_back, two_back), PLACES_WITH) if w == (number, axis)]
            for axis in range(2)
        ])

    def before(h, *stages):
        return sum((got[stage][h] for stage in stages), [])

    each("far", False, lambda half, h: send_far(line, half, flat))
    each("raw", False, lambda half, h: send_raw(line, half, flat))
    each("near", False, lambda half, h: send_near(line, half, flat, *before(h, "far")))
    each("far2", True, lambda half, h: send_far2(line, half, flat, before(h, "raw", "near")))
    for number, (first, end) in enumerate(spaces):
        each(
            number, True,
            lambda half, h: send_near2(
                line, half, flat, before(h, "raw", "near"), before(h, "far2"), first // TILE, (end - first) // TILE
            ),
        )
    fresh = update = None
    lists, mine = {}, {}
    for what, number in TAIL:
        number = int(number)
        first, end = spaces[number]
        piece = Part(pair, first, end - first, dict(f=FINE, s=TILE, j=BROAD)[what])
        if what == "f":
            full = [before(h, "raw", "near", number) for h in range(2)]
            fresh, own = finish(line, piece, flat, momentum, positions, full, tables, fresh)
            lists[number] = [own] + [along_z(own, step) for step in (1, -1, 2)]
        elif what == "s":
            part = spread(line, piece, lists[number], places, tables[1])
            mine[number] = part, other_core(part)
        else:
            update = join(line, piece, *mine[number], spans, update)
    return update, fresh


def solution(mesh):
    placed = (P("rep", "fsdp", None, None), P("rep", None, "fsdp"), P("rep", None, "fsdp"))
    return jax.shard_map(
        on_device,
        mesh=mesh,
        in_specs=placed,
        out_specs=(P(None, "fsdp"), P("rep", None, "fsdp")),
        check_vma=False,
    )
```
